32 devices in a mesh: ev: 4 (over z), site: 8 (over y, x, core).
Axes of the slice: x: 2, y: 2, z: 4, core: 2. Of those that a mesh axis runs over, the one named last changes fastest.
Arguments:
- ruptures: float32 [6, 64], P(None, ('ev', 'site')), may hold values from -60 to 260, as said below
- event_rupture: int32 [32], P(('ev', 'site')), may hold values from 0 to 63
- epsilon: bfloat16 [2, 32, 4096], P(None, ('ev', 'site')), may hold values from -4 to 4
- site_coords: float32 [2, 4096], replicated, may hold values from 0 to 200
- vulnerability: bfloat16 [128, 40], replicated, may hold values from 0 to 1
- taxo_measure: int32 [128], replicated, may hold values from 0 to 1
- taxo_offset: int32 [128], replicated, may hold values from 0 to 24
- asset_site: int32 [81920], P('site'), may hold values from 0 to 511
- asset_taxo: int32 [81920], P('site'), may hold values from 0 to 127
- asset_tract: int32 [81920], P('site'), may hold values from 0 to 7
- asset_value: float32 [81920], P('site'), may hold values from 0.002 to 0.05
Outputs:
- losses: float32 [8, 32, 128], P('site', 'ev')
The draws below stay inside these ranges and needn't reach their ends.
Inputs may be any that keep to these rules, and one draw needn't show every extreme that they name: Asset a stands at site (a // 10240) * 512 + asset_site[a]. `ruptures`: every rupture is 5 km long or more, its depth 2 to 20 km and its magnitude 5 to 8.
All inputs are finite; a program needn't handle non-finite values.
Results may differ from the reference program's by a relative error of at most 0.00064.
Values may be sent and summed in bfloat16 or wider, within the bound.
No kernel may reach another device: no remote copies, remote signals or barrier semaphores. Data moves between devices by JAX's collectives and lax.ppermute only.
A program may use at most 128 MiB of HBM per device.

```python
import math
import jax
import jax.numpy as jnp
import numpy as np
from jax import lax

SITE_DEV = 512
ASSET_DEV = 10240
TAXO = 128
G = 64
NB = 40
EVENTS = 32
SITES = 4096
ASSETS = 81920
RUPTURES = 64
TRACTS = 8
N_SITE = 8


def draw_ruptures(key, part):
    keys = jax.random.split(jax.random.fold_in(key, 11), 6)
    start_x = jax.random.uniform(keys[0], (RUPTURES,), jnp.float32, 0.0, 200.0)
    start_y = jax.random.uniform(keys[1], (RUPTURES,), jnp.float32, 0.0, 200.0)
    heading = jax.random.uniform(keys[2], (RUPTURES,), jnp.float32, -math.pi, math.pi)
    spread_len = jax.random.uniform(keys[3], (RUPTURES,), jnp.float32, 0.0, 1.0)
    rup_depth = jax.random.uniform(keys[4], (RUPTURES,), jnp.float32, 2.0, 20.0)
    spread_mag = jax.random.uniform(keys[5], (RUPTURES,), jnp.float32, 0.0, 1.0)
    seg_length = 5.0 + 55.0 * spread_len
    magnitude = 5.0 + 3.0 * spread_mag
    end_x = start_x + seg_length * jnp.cos(heading)
    end_y = start_y + seg_length * jnp.sin(heading)
    return jnp.stack([start_x, start_y, end_x, end_y, rup_depth, magnitude]).astype(jnp.float32)


def set_ends(result, key, least, top_value):
    longest = result.shape.index(max(result.shape))
    spots = []
    for shift in (0, 1):
        where = [jax.random.randint(jax.random.fold_in(key, axis), (), 0, length) for axis, length in enumerate(result.shape)]
        where[longest] = (where[longest] + shift) % result.shape[longest]
        spots.append(tuple(where))
    return result.at[spots[0]].set(least).at[spots[1]].set(top_value)


def steps_of(own_key, shape, cuts, smallest, high):
    def one(axis_at, parts):
        draws = jax.random.uniform(jax.random.fold_in(jax.random.fold_in(own_key, 6), axis_at), (parts,), jnp.float32, smallest / len(cuts), high / len(cuts))
        return jnp.repeat(jnp.exp(draws), shape[axis_at] // parts).reshape((-1,) + (1,) * (len(shape) - axis_at - 1))

    gain = one(*cuts[0])
    for cut in cuts[1:]:
        gain = gain * one(*cut)
    return gain


def rank_bounds(count, slope):
    loads = [(1 << 20) // math.isqrt(grade ** slope) + 1 for grade in range(1, count + 1)]
    width = 1 + sum(loads) // (1 << 30)
    return np.cumsum(np.array([max(1, weight // width) for weight in loads]))


def ranked(own_key, extent, amount, slope):
    grid = rank_bounds(amount, slope)
    lot = jax.random.randint(jax.random.fold_in(own_key, 1), extent, 0, int(grid[amount - 1]))
    rank = jnp.searchsorted(jnp.asarray(grid, jnp.int32), lot, side="right")
    return jax.random.permutation(jax.random.fold_in(own_key, 2), amount)[rank].astype(jnp.int32)


def normal_values(rng, shape, width, most, pieces=(), held_as=jnp.bfloat16):
    drawn = width * jax.random.normal(rng, shape, jnp.float32)
    if pieces:
        drawn = drawn * steps_of(rng, shape, pieces, -0.22, 0.18)
    return jnp.clip(drawn, -most, most).astype(held_as)


def setup_inputs(seed: int = 0) -> dict:
    splits = jax.random.split(jax.random.key(seed), 12)
    ruptures = draw_ruptures(jax.random.fold_in(splits[11], 71), 0)
    event_rupture = set_ends(jax.random.randint(splits[1], (EVENTS,), 0, RUPTURES), jax.random.fold_in(splits[1], 1), 0, RUPTURES - 1).astype(jnp.int32)
    epsilon = normal_values(splits[2], (2, EVENTS, SITES), 1.0, 4.0, ((1, 32),))
    site_coords = jnp.clip(jax.random.uniform(splits[3], (2, SITES), jnp.float32, 0.0, 200.0), 0.0, 200.0)
    vulnerability = jnp.clip(jax.random.uniform(splits[4], (TAXO, NB), jnp.float32, 0.0, 1.0), 0.0, 1.0).astype(jnp.bfloat16)
    taxo_measure = set_ends(jax.random.randint(splits[5], (TAXO,), 0, 2), jax.random.fold_in(splits[5], 1), 0, 1).astype(jnp.int32)
    taxo_offset = set_ends(jax.random.randint(splits[6], (TAXO,), 0, G - NB + 1), jax.random.fold_in(splits[6], 1), 0, G - NB).astype(jnp.int32)
    asset_site = set_ends(ranked(splits[7], (ASSETS,), SITE_DEV, 2), jax.random.fold_in(splits[7], 3), 0, SITE_DEV - 1).astype(jnp.int32)
    asset_taxo = set_ends(ranked(splits[8], (ASSETS,), TAXO, 1), jax.random.fold_in(splits[8], 3), 0, TAXO - 1).astype(jnp.int32)
    asset_tract = set_ends(jax.random.randint(splits[9], (ASSETS,), 0, TRACTS), jax.random.fold_in(splits[9], 1), 0, TRACTS - 1).astype(jnp.int32)
    asset_value = jnp.clip(jnp.exp(math.log(0.05) - 3.218876 * jax.random.uniform(splits[10], (ASSETS,), jnp.float32) ** steps_of(splits[10], (ASSETS,), ((0, 8),), -0.2, 0.2)), 0.002, 0.05)
    return {"ruptures": ruptures, "event_rupture": event_rupture, "epsilon": epsilon, "site_coords": site_coords, "vulnerability": vulnerability, "taxo_measure": taxo_measure, "taxo_offset": taxo_offset, "asset_site": asset_site, "asset_taxo": asset_taxo, "asset_tract": asset_tract, "asset_value": asset_value}


COEFFS = ((1.0, 1.1, 1.0, 6.0, 0.004, 0.6), (0.3, 1.4, 0.9, 8.0, 0.002, 0.7))
LOW_LEVEL = -6.0
LEVEL_STEP = 0.1

def intensity(geometry, coords, epsilon):
    start_x = geometry[0][:, None]
    start_y = geometry[1][:, None]
    along_x = (geometry[2] - geometry[0])[:, None]
    along_y = (geometry[3] - geometry[1])[:, None]
    rup_depth = geometry[4][:, None]
    magnitude = geometry[5][:, None]
    rel_x = coords[0][None, :] - start_x
    rel_y = coords[1][None, :] - start_y
    length_sq = along_x * along_x + along_y * along_y
    portion = jnp.clip((rel_x * along_x + rel_y * along_y) / length_sq, 0.0, 1.0)
    off_x = rel_x - portion * along_x
    off_y = rel_y - portion * along_y
    distance = jnp.sqrt(off_x * off_x + off_y * off_y + rup_depth * rup_depth)
    results = []
    for measure in range(2):
        coeffs = COEFFS[measure]
        value = coeffs[0] + coeffs[1] * (magnitude - 6.0) - coeffs[2] * 0.5 * jnp.log(distance * distance + coeffs[3] * coeffs[3]) - coeffs[4] * distance + coeffs[5] * epsilon[measure].astype(jnp.float32)
        results.append(value)
    return jnp.stack(results)

def tent_weights(fields):
    position = jnp.clip((fields - LOW_LEVEL) / LEVEL_STEP, 0.0, G - 1.0)
    levels = jnp.arange(G, dtype=jnp.float32)
    weights = jnp.maximum(0.0, 1.0 - jnp.abs(position[..., None] - levels))
    n_events = fields.shape[1]
    n_sites = fields.shape[2]
    return weights.transpose(1, 2, 0, 3).reshape(n_events * n_sites, 2 * G).astype(jnp.bfloat16)

def curves(vulnerability, taxo_measure, taxo_offset):
    level_rows = jnp.arange(G, dtype=jnp.int32)[:, None] - taxo_offset[None, :]
    point_index = jnp.clip(level_rows, 0, NB - 1).astype(jnp.int32)
    curve_rows = jnp.take_along_axis(vulnerability.T, point_index, axis=0)
    blank = jnp.zeros_like(curve_rows)
    curve_rows = jnp.where(level_rows >= 0, curve_rows, blank)
    first_half = jnp.where(taxo_measure[None, :] == 0, curve_rows, blank)
    second_half = jnp.where(taxo_measure[None, :] == 1, curve_rows, blank)
    return jnp.concatenate([first_half, second_half], axis=0)

def build_exposure(asset_site, asset_taxo, asset_tract, asset_value, site_count, tracts):
    flat_index = ((asset_taxo * site_count + asset_site) * tracts + asset_tract).astype(jnp.int32)
    summed = jnp.zeros((TAXO * site_count * tracts,), jnp.float32).at[flat_index].add(asset_value)
    return summed.reshape(TAXO, site_count, tracts).astype(jnp.bfloat16)

def reference(ruptures, event_rupture, epsilon, site_coords, vulnerability, taxo_measure, taxo_offset, asset_site, asset_taxo, asset_tract, asset_value):
    geometry = jnp.take(ruptures, event_rupture, axis=1)
    curve_table = curves(vulnerability, taxo_measure, taxo_offset)
    ev_block = min(128, EVENTS)

    def per_shard(running, shard_index):
        site_first = (shard_index * SITE_DEV).astype(jnp.int32)
        asset_first = (shard_index * ASSET_DEV).astype(jnp.int32)
        own_coords = lax.dynamic_slice_in_dim(site_coords, site_first, SITE_DEV, 1)
        exposure = build_exposure(lax.dynamic_slice_in_dim(asset_site, asset_first, ASSET_DEV, 0), lax.dynamic_slice_in_dim(asset_taxo, asset_first, ASSET_DEV, 0), lax.dynamic_slice_in_dim(asset_tract, asset_first, ASSET_DEV, 0), lax.dynamic_slice_in_dim(asset_value, asset_first, ASSET_DEV, 0), SITE_DEV, TRACTS)
        exposure_wide = exposure.astype(jnp.float32)

        def per_block(inner, block_index):
            first_row = (block_index * ev_block).astype(jnp.int32)
            event_geo = lax.dynamic_slice_in_dim(geometry, first_row, ev_block, 1)
            eps_block = lax.dynamic_slice(epsilon, (jnp.int32(0), first_row, site_first), (2, ev_block, SITE_DEV))
            fields = intensity(event_geo, own_coords, eps_block)
            loss_ratio = jnp.dot(tent_weights(fields), curve_table, preferred_element_type=jnp.float32)
            loss_ratio = loss_ratio.astype(jnp.bfloat16).reshape(ev_block, SITE_DEV, TAXO)
            term = jnp.einsum('bst,tsr->rbt', loss_ratio.astype(jnp.float32), exposure_wide)
            before = lax.dynamic_slice_in_dim(inner, first_row, ev_block, 1)
            return (lax.dynamic_update_slice_in_dim(inner, before + term, first_row, 1), None)
        running, _ = lax.scan(per_block, running, jnp.arange(EVENTS // ev_block, dtype=jnp.int32))
        return (running, None)
    losses = jnp.zeros((TRACTS, EVENTS, TAXO), jnp.float32)
    losses, _ = lax.scan(per_shard, losses, jnp.arange(N_SITE, dtype=jnp.int32))
    return losses
```

```python
import jax
import jax.numpy as jnp
from jax import lax
from jax.experimental import pallas as pl
from jax.experimental.pallas import tpu as pltpu
from jax.sharding import PartitionSpec as P

SITE_DEV = 512
TAXO = 128
G = 64
NB = 40
LANES = 128
ROWS = 8

COEFFS = ((1.0, 1.1, 1.0, 6.0, 0.004, 0.6), (0.3, 1.4, 0.9, 8.0, 0.002, 0.7))
LOW_LEVEL = -6.0
LEVEL_STEP = 0.1

AXES = ("ev", "site")
F32 = jnp.float32
BF16 = jnp.bfloat16
NT = (((1,), (1,)), ((), ()))

VMEM = pl.BlockSpec(memory_space=pltpu.VMEM)
SMEM = pl.BlockSpec(memory_space=pltpu.SMEM)


def params():
    return pltpu.CompilerParams(vmem_limit_bytes=40 << 20)


def pack_kernel(n_ev, n_site, rup_ref, idx_ref, eps_ref, out_ref):
    n_rup = rup_ref.shape[1]
    lane = lax.broadcasted_iota(jnp.int32, (2, LANES), 1)
    row = jnp.zeros((2, LANES), F32)
    for b in range(n_rup):
        for c in range(6):
            row = jnp.where(lane == 6 * b + c, rup_ref[c, b], row)
    row = jnp.where(lane == 6 * n_rup, idx_ref[0].astype(F32), row)
    eps = eps_ref[...].astype(F32)

    def fill(i, carry):
        for j in range(n_site):
            out_ref[i * n_site + j, :, :SITE_DEV] = eps[:, j * SITE_DEV : (j + 1) * SITE_DEV]
            out_ref[i * n_site + j, :, SITE_DEV:] = row
        return carry

    lax.fori_loop(0, n_ev, fill, 0, unroll=n_ev <= 4)


def exposure_kernel(
    t_dev, rows, site_ref, taxo_ref, tract_ref, value_ref, vul_ref, measure_ref, offset_ref,
    exp_ref, curve_ref, site_s, col_s, high_s, low_s, sum_s, curve_s,
):
    me = lax.axis_index("ev")
    first = me * t_dev
    taxo = taxo_ref[...] - first
    own = (taxo >= 0) & (taxo < t_dev)
    value = value_ref[...]
    high = value.astype(BF16).astype(F32)
    site_s[...] = site_ref[...].astype(F32)
    col_s[...] = jnp.where(own, tract_ref[...] * t_dev + taxo, -1).astype(F32)
    high_s[...] = high
    low_s[...] = value - high

    n_col = exp_ref.shape[1]
    level = lax.broadcasted_iota(jnp.int32, (256, LANES), 0).astype(F32).astype(BF16)
    zero = jnp.zeros((256, LANES), BF16)
    one = jnp.ones((256, LANES), BF16)

    def spread(ref, q, less=0.0):
        return jnp.broadcast_to((ref[pl.ds(q, 1), :] - less).astype(BF16), (256, LANES))

    def beside(parts):
        return jnp.concatenate(parts, axis=1)

    sum_s[...] = jnp.zeros_like(sum_s)

    def step(c, carry):
        site_rows = [[] for _ in range(SITE_DEV // 256)]
        high_rows, low_rows = [], []
        for u in range(rows):
            q = c * rows + u
            for part, found in enumerate(site_rows):
                found.append(jnp.where(level == spread(site_s, q, 256.0 * part), one, zero))
            here = level == spread(col_s, q)
            high_rows.append(jnp.where(here, spread(high_s, q), zero))
            low_rows.append(jnp.where(here, spread(low_s, q), zero))
        at_site = jnp.concatenate([beside(found) for found in site_rows], axis=0)
        sum_s[...] += lax.dot_general(
            beside([at_site, at_site]), beside(high_rows + low_rows), NT, preferred_element_type=F32
        )
        return carry

    lax.fori_loop(0, site_s.shape[0] // rows, step, 0)
    exp_ref[...] = sum_s[...].astype(BF16)

    vul = vul_ref[...].astype(F32)
    table = jnp.concatenate([vul, jnp.broadcast_to(vul[NB - 1 : NB], (G - NB, TAXO))], axis=0)
    offset = jnp.broadcast_to(offset_ref[...], (G, TAXO))
    level_row = lax.broadcasted_iota(jnp.int32, (G, TAXO), 0)
    for bit in range(5):
        size = 1 << bit
        moved = jnp.where(level_row >= size, pltpu.roll(table, size, 0), 0.0)
        table = jnp.where((offset & size) != 0, moved, table)
    measure = jnp.broadcast_to(measure_ref[...], (G, TAXO))
    both = jnp.concatenate(
        [jnp.where(measure == 0, table, 0.0), jnp.where(measure == 1, table, 0.0)], axis=0
    )
    curve_s[...] = both.T
    curve_ref[...] = curve_s[pl.ds(pl.multiple_of(first, ROWS), t_dev), :].astype(BF16)


def swap_groups(block, groups, width):
    total = block.shape[0]
    high = total // groups
    row_group = lax.broadcasted_iota(jnp.int32, block.shape, 0) // high
    lane_group = lax.broadcasted_iota(jnp.int32, block.shape, 1) // width
    result = block
    for d in range(1, groups):
        moved = pltpu.roll(pltpu.roll(block, total - high * d, 0), width * d, 1)
        gap = lane_group - row_group
        result = jnp.where((gap == d) | (gap == d - groups), moved, result)
    return result


def loss_kernel(n_ev, n_site, n_rup, got_ref, coords_ref, exp_ref, curve_ref, out_ref, geo_s, ratio_s, loss_s):
    n_dev = n_ev * n_site
    t_dev = curve_ref.shape[0]
    n_col = exp_ref.shape[1]
    events = n_dev
    ev_dev = events // n_ev
    me = lax.axis_index("site")
    start = pl.multiple_of(me * SITE_DEV, LANES)
    x = jnp.broadcast_to(coords_ref[0:1, pl.ds(start, SITE_DEV)], (ROWS, SITE_DEV))
    y = jnp.broadcast_to(coords_ref[1:2, pl.ds(start, SITE_DEV)], (ROWS, SITE_DEV))

    def take_geometry(b, carry):
        rows = [got_ref[b * ROWS + u, :, SITE_DEV:][0:1] for u in range(ROWS)]
        geo_s[pl.ds(pl.multiple_of(b * ROWS, ROWS), ROWS), :] = jnp.concatenate(rows, axis=0)
        return carry

    lax.fori_loop(0, n_dev // ROWS, take_geometry, 0, unroll=n_dev // ROWS <= 4)
    every = geo_s[...]
    high = every.astype(BF16)
    rest = every - high.astype(F32)
    middle = rest.astype(BF16)
    low = (rest - middle.astype(F32)).astype(BF16)
    level = lax.broadcasted_iota(jnp.int32, (G, SITE_DEV), 0).astype(F32).astype(BF16)
    level_less = (lax.broadcasted_iota(jnp.int32, (G, SITE_DEV), 0) - 1).astype(F32).astype(BF16)
    zero = jnp.zeros((G, SITE_DEV), BF16)
    curve = curve_ref[...]
    exposure = exp_ref[...]
    diagonal = lax.broadcasted_iota(jnp.int32, (t_dev, n_col), 0) == (
        lax.broadcasted_iota(jnp.int32, (t_dev, n_col), 1) % t_dev
    )

    def block(b, carry):
        first = pl.multiple_of(b * ROWS, ROWS)
        rupture = geo_s[pl.ds(first, ROWS), :][:, 6 * n_rup : 6 * n_rup + 1].astype(jnp.int32)
        owner = rupture // n_rup
        hot = (lax.broadcasted_iota(jnp.int32, (ROWS, n_dev), 1) == owner).astype(BF16)
        found = (
            jnp.dot(hot, high, preferred_element_type=F32)
            + jnp.dot(hot, middle, preferred_element_type=F32)
        ) + jnp.dot(hot, low, preferred_element_type=F32)
        own = found
        for u in range(1, n_rup):
            own = jnp.where(rupture - owner * n_rup == u, pltpu.roll(found, LANES - 6 * u, 1), own)
        start_x = own[:, 0:1]
        start_y = own[:, 1:2]
        along_x = own[:, 2:3] - start_x
        along_y = own[:, 3:4] - start_y
        depth = own[:, 4:5]
        size = own[:, 5:6]
        length_sq = along_x * along_x + along_y * along_y
        rel_x = x - start_x
        rel_y = y - start_y
        portion = jnp.clip((rel_x * along_x + rel_y * along_y) / length_sq, 0.0, 1.0)
        off_x = rel_x - portion * along_x
        off_y = rel_y - portion * along_y
        squared = off_x * off_x + off_y * off_y + depth * depth
        distance = jnp.sqrt(squared)
        got = [got_ref[b * ROWS + u, :, :SITE_DEV] for u in range(ROWS)]
        below, weight_0, weight_1 = [], [], []
        for k in range(2):
            c = COEFFS[k]
            eps = jnp.concatenate([rows[k : k + 1] for rows in got], axis=0)
            field = (
                c[0] + c[1] * (size - 6.0)
                - c[2] * 0.5 * jnp.log(distance * distance + c[3] * c[3])
                - c[4] * distance
                + c[5] * eps
            )
            position = jnp.clip((field - LOW_LEVEL) / LEVEL_STEP, 0.0, G - 1.0)
            floor = jnp.floor(position)
            below.append(floor)
            weight_0.append(1.0 - (position - floor))
            weight_1.append(jnp.maximum(0.0, 1.0 - ((floor + 1.0) - position)))

        def wide(array, e):
            return jnp.broadcast_to(array[e : e + 1].astype(BF16), (G, SITE_DEV))

        for e in range(ROWS):
            tents = []
            for k in range(2):
                at = wide(below[k], e)
                tents.append(
                    jnp.where(
                        level == at,
                        wide(weight_0[k], e),
                        jnp.where(level_less == at, wide(weight_1[k], e), zero),
                    )
                )
            ratio = jnp.dot(curve, jnp.concatenate(tents, axis=0), preferred_element_type=F32)
            ratio_s[e * t_dev : (e + 1) * t_dev, :] = ratio
        terms = jnp.dot(ratio_s[...].astype(BF16), exposure, preferred_element_type=F32)
        rows = [
            jnp.sum(jnp.where(diagonal, terms[e * t_dev : (e + 1) * t_dev], 0.0), axis=0, keepdims=True)
            for e in range(ROWS)
        ]
        loss_s[pl.ds(first, ROWS), :] = jnp.concatenate(rows, axis=0)
        return carry

    lax.fori_loop(0, events // ROWS, block, 0)

    halves = n_col // LANES

    def arrange(i, carry):
        first = pl.multiple_of(i * ev_dev, ROWS)
        for u in range(halves):
            part = loss_s[pl.ds(first, ev_dev), u * LANES : (u + 1) * LANES]
            out_ref[pl.ds(pl.multiple_of((i * halves + u) * ev_dev, ROWS), ev_dev), :] = swap_groups(
                part, n_ev, t_dev
            )
        return carry

    lax.fori_loop(0, n_ev, arrange, 0, unroll=n_ev <= 4)


def total_kernel(n_ev, n_site, got_ref, out_ref):
    high = got_ref.shape[0] // (n_ev * n_site)
    rows = []
    for i in range(n_ev):
        for h in range(high):
            part = got_ref[pl.ds(i * n_site * high + h, n_site, stride=high), :]
            rows.append(jnp.sum(part, axis=0, keepdims=True))
    out_ref[...] = swap_groups(jnp.concatenate(rows, axis=0), n_ev, LANES // n_ev)


def shards(
    ruptures,
    event_rupture,
    epsilon,
    site_coords,
    vulnerability,
    taxo_measure,
    taxo_offset,
    asset_site,
    asset_taxo,
    asset_tract,
    asset_value,
):
    n_ev = lax.axis_size("ev")
    n_site = lax.axis_size("site")
    n_dev = n_ev * n_site
    n_rup = ruptures.shape[1]
    sites = epsilon.shape[2]
    t_dev = TAXO // n_ev
    n_col = n_site * t_dev
    asset_rows = asset_site.shape[0] // LANES

    def exchange(array):
        return lax.all_to_all(array, AXES, split_axis=0, concat_axis=0, tiled=True)

    packed = pl.pallas_call(
        lambda *refs: pack_kernel(n_ev, n_site, *refs),
        out_shape=jax.ShapeDtypeStruct((n_dev, 2, SITE_DEV + LANES), F32),
        in_specs=[SMEM, SMEM, VMEM],
        out_specs=VMEM,
        compiler_params=params(),
    )(ruptures, event_rupture, epsilon.reshape(2, sites))
    got = exchange(packed)

    def as_rows(array):
        return array.reshape(asset_rows, LANES)

    exposure, curve = pl.pallas_call(
        lambda *refs: exposure_kernel(t_dev, 20, *refs),
        out_shape=(
            jax.ShapeDtypeStruct((SITE_DEV, n_col), BF16),
            jax.ShapeDtypeStruct((t_dev, 2 * G), BF16),
        ),
        in_specs=[VMEM] * 7,
        out_specs=(VMEM, VMEM),
        scratch_shapes=[pltpu.VMEM((asset_rows, LANES), F32)] * 4
        + [pltpu.VMEM((SITE_DEV, n_col), F32), pltpu.VMEM((TAXO, 2 * G), F32)],
        compiler_params=params(),
        cost_estimate=pl.CostEstimate(
            flops=4 * asset_rows * LANES * SITE_DEV * n_col, bytes_accessed=1 << 20, transcendentals=0
        ),
    )(
        as_rows(asset_site),
        as_rows(asset_taxo),
        as_rows(asset_tract),
        as_rows(asset_value),
        vulnerability.T,
        taxo_measure.reshape(1, TAXO),
        taxo_offset.reshape(1, TAXO),
    )

    parts = pl.pallas_call(
        lambda *refs: loss_kernel(n_ev, n_site, n_rup, *refs),
        out_shape=jax.ShapeDtypeStruct((n_dev * n_col // LANES, LANES), F32),
        in_specs=[VMEM] * 4,
        out_specs=VMEM,
        scratch_shapes=[
            pltpu.VMEM((n_dev, LANES), F32),
            pltpu.VMEM((ROWS * t_dev, SITE_DEV), F32),
            pltpu.VMEM((n_dev, n_col), F32),
        ],
        compiler_params=params(),
    )(got, site_coords, exposure, curve)

    losses = pl.pallas_call(
        lambda *refs: total_kernel(n_ev, n_site, *refs),
        out_shape=jax.ShapeDtypeStruct((n_dev // n_ev, LANES), F32),
        in_specs=[VMEM],
        out_specs=VMEM,
        compiler_params=params(),
    )(exchange(parts))
    return losses[None]


def solution(mesh):
    in_specs = (
        P(None, ("ev", "site")),
        P(("ev", "site")),
        P(None, ("ev", "site"), None),
        P(),
        P(),
        P(),
        P(),
        P("site"),
        P("site"),
        P("site"),
        P("site"),
    )
    out_specs = P("site", "ev", None)
    return jax.shard_map(shards, mesh=mesh, in_specs=in_specs, out_specs=out_specs, check_vma=False)
```

```python
import jax
import jax.numpy as jnp
from jax import lax
from jax.experimental import pallas as pl
from jax.experimental.pallas import tpu as pltpu
from jax.sharding import PartitionSpec as P

SITE_DEV = 512
TAXO = 128
G = 64
NB = 40
LANES = 128
ROWS = 8
PART = 16
EVENT_BLOCK = 32
CODES = 1 << 17
SLANT = 13
HOLE = 1 << 24
COMPACT_ROWS = 16

COEFFS = ((1.0, 1.1, 1.0, 6.0, 0.004, 0.6), (0.3, 1.4, 0.9, 8.0, 0.002, 0.7))
LOW_LEVEL = -6.0
LEVEL_STEP = 0.1

AXES = ("ev", "site")
F32 = jnp.float32
BF16 = jnp.bfloat16
NT = (((1,), (1,)), ((), ()))

VMEM = pl.BlockSpec(memory_space=pltpu.VMEM)
HBM = pl.BlockSpec(memory_space=pltpu.HBM)


def params(mebibytes):
    return pltpu.CompilerParams(vmem_limit_bytes=mebibytes << 20)


def parts_of(value):
    high = value.astype(BF16).astype(F32)
    rest = value - high
    middle = rest.astype(BF16).astype(F32)
    return high, middle, (rest - middle).astype(BF16).astype(F32)


def pack_kernel(n_ev, n_site, rup_hbm, idx_hbm, eps_hbm, out_ref, rup_ref, idx_ref, eps_ref, sems):
    copies = [
        pltpu.make_async_copy(source, target, sems.at[k])
        for k, (source, target) in enumerate(((rup_hbm, rup_ref), (idx_hbm, idx_ref), (eps_hbm, eps_ref)))
    ]
    for copy in copies:
        copy.start()
    n_rup = rup_ref.shape[0]
    lane = lax.broadcasted_iota(jnp.int32, (2, LANES), 1)
    row = jnp.zeros((2, LANES), F32)
    copies[0].wait()
    copies[1].wait()
    for b in range(n_rup):
        for c in range(6):
            row = jnp.where(lane == 6 * b + c, rup_ref[b, c], row)
    row = jnp.where(lane == 6 * n_rup, idx_ref[0].astype(F32), row)
    high, middle, low = parts_of(row)
    row = (high + pltpu.roll(middle, PART, 1) + pltpu.roll(low, 2 * PART, 1)).astype(BF16)
    copies[2].wait()
    eps = eps_ref[...]

    def fill(i, carry):
        for j in range(n_site):
            out_ref[i * n_site + j, :, :SITE_DEV] = eps[:, j * SITE_DEV : (j + 1) * SITE_DEV]
            out_ref[i * n_site + j, :, SITE_DEV:] = row
        return carry

    lax.fori_loop(0, n_ev, fill, 0, unroll=n_ev <= 4)


def compact(own, code, value):
    rows = own.shape[0]
    above = lax.broadcasted_iota(jnp.int32, (rows, rows), 1) < lax.broadcasted_iota(jnp.int32, (rows, rows), 0)
    gaps = jnp.dot(above.astype(BF16), 1.0 - own.astype(BF16), preferred_element_type=F32).astype(jnp.int32)
    word = jnp.where(own, gaps * CODES + code, HOLE)
    size = 1
    while size < rows:
        bit = size * CODES
        from_word = jnp.concatenate([word[size:], jnp.full((size, LANES), HOLE, jnp.int32)], axis=0)
        from_value = jnp.concatenate([value[size:], jnp.zeros((size, LANES), F32)], axis=0)
        comes = (from_word & bit) != 0
        value = jnp.where(comes, from_value, value)
        word = jnp.where(comes, from_word, jnp.where((word & bit) != 0, HOLE, word))
        size *= 2
    return word, value


def slanted(array):
    return jnp.concatenate(
        [
            pltpu.roll(array[q : q + ROWS], (11 * q // ROWS) % 36, 1, stride=SLANT, stride_axis=0)
            for q in range(0, array.shape[0], ROWS)
        ],
        axis=0,
    )


def exposure_kernel(
    t_dev, rows, site_ref, taxo_ref, tract_ref, value_ref, vul_hbm, measure_hbm, offset_hbm,
    exp_ref, curve_ref, site_s, col_s, high_s, low_s, sum_s, curve_s, vul_ref, measure_ref, offset_ref, sems,
):
    copies = [
        pltpu.make_async_copy(source, target, sems.at[k])
        for k, (source, target) in enumerate(
            ((vul_hbm, vul_ref), (measure_hbm, measure_ref), (offset_hbm, offset_ref))
        )
    ]
    for copy in copies:
        copy.start()
    me = lax.axis_index("ev")
    first = me * t_dev
    n_col = exp_ref.shape[1]
    taxo = taxo_ref[...] - first
    own = (taxo >= 0) & (taxo < t_dev)
    code = site_ref[...] * n_col + tract_ref[...] * t_dev + taxo
    word, value = compact(own, code, value_ref[...])
    word, value = slanted(word), slanted(value)
    own = word != HOLE
    most = jnp.max(jnp.sum(own.astype(F32), axis=0, keepdims=True)).astype(jnp.int32)
    word, value = compact(own, word & (CODES - 1), value)
    high = value.astype(BF16).astype(F32)
    site_s[...] = ((word & (CODES - 1)) // n_col).astype(F32)
    col_s[...] = jnp.where((word & HOLE) != 0, -1, word & (n_col - 1)).astype(F32)
    high_s[...] = high
    low_s[...] = value - high

    level = lax.broadcasted_iota(jnp.int32, (256, LANES), 0).astype(F32).astype(BF16)
    zero = jnp.zeros((256, LANES), BF16)
    one = jnp.ones((256, LANES), BF16)

    def spread(ref, q, less=0.0):
        return jnp.broadcast_to((ref[pl.ds(q, 1), :] - less).astype(BF16), (256, LANES))

    def beside(parts):
        return jnp.concatenate(parts, axis=1)

    sum_s[...] = jnp.zeros_like(sum_s)

    def step(c, carry):
        site_rows = [[] for _ in range(SITE_DEV // 256)]
        high_rows, low_rows = [], []
        for u in range(rows):
            q = c * rows + u
            for part, found in enumerate(site_rows):
                found.append(jnp.where(level == spread(site_s, q, 256.0 * part), one, zero))
            here = level == spread(col_s, q)
            high_rows.append(jnp.where(here, spread(high_s, q), zero))
            low_rows.append(jnp.where(here, spread(low_s, q), zero))
        at_site = jnp.concatenate([beside(found) for found in site_rows], axis=0)
        sum_s[...] += lax.dot_general(
            beside([at_site, at_site]), beside(high_rows + low_rows), NT, preferred_element_type=F32
        )
        return carry

    lax.fori_loop(0, (most + rows - 1) // rows, step, 0)
    exp_ref[...] = sum_s[...].astype(BF16)

    for copy in copies:
        copy.wait()
    vul = vul_ref[...].astype(F32)
    table = jnp.concatenate([vul, jnp.broadcast_to(vul[NB - 1 : NB], (G - NB, TAXO))], axis=0)
    offset = jnp.broadcast_to(offset_ref[...], (G, TAXO))
    level_row = lax.broadcasted_iota(jnp.int32, (G, TAXO), 0)
    for bit in range(5):
        size = 1 << bit
        moved = jnp.where(level_row >= size, pltpu.roll(table, size, 0), 0.0)
        table = jnp.where((offset & size) != 0, moved, table)
    measure = jnp.broadcast_to(measure_ref[...], (G, TAXO))
    both = jnp.concatenate(
        [jnp.where(measure == 0, table, 0.0), jnp.where(measure == 1, table, 0.0)], axis=0
    )
    curve_s[...] = both.T
    curve_ref[...] = curve_s[pl.ds(pl.multiple_of(first, ROWS), t_dev), :].astype(BF16)


def swap_groups(block, groups, width):
    total = block.shape[0]
    high = total // groups
    row_group = lax.broadcasted_iota(jnp.int32, block.shape, 0) // high
    lane_group = lax.broadcasted_iota(jnp.int32, block.shape, 1) // width
    result = block
    for d in range(1, groups):
        moved = pltpu.roll(pltpu.roll(block, total - high * d, 0), width * d, 1)
        gap = lane_group - row_group
        result = jnp.where((gap == d) | (gap == d - groups), moved, result)
    return result


def loss_kernel(n_ev, n_site, n_rup, got_ref, coords_ref, exp_ref, curve_ref, out_ref, geo_s, ratio_s, loss_s):
    n_dev = n_ev * n_site
    t_dev = curve_ref.shape[0]
    n_col = exp_ref.shape[1]
    events = n_dev
    ev_dev = events // n_ev
    me = lax.axis_index("site")
    start = pl.multiple_of(me * SITE_DEV, LANES)
    x = coords_ref[0:1, pl.ds(start, SITE_DEV)]
    y = coords_ref[1:2, pl.ds(start, SITE_DEV)]

    def take_geometry(b, carry):
        first = b * EVENT_BLOCK
        rows = [got_ref[first + u, :, SITE_DEV:].astype(F32)[0:1] for u in range(EVENT_BLOCK)]
        geo_s[pl.ds(pl.multiple_of(first, ROWS), EVENT_BLOCK), :] = jnp.concatenate(rows, axis=0)
        return carry

    lax.fori_loop(0, n_dev // EVENT_BLOCK, take_geometry, 0)
    ruptures = geo_s[...].astype(BF16)
    level = lax.broadcasted_iota(jnp.int32, (G, SITE_DEV), 0).astype(F32).astype(BF16)
    level_less = (lax.broadcasted_iota(jnp.int32, (G, SITE_DEV), 0) - 1).astype(F32).astype(BF16)
    zero = jnp.zeros((G, SITE_DEV), BF16)
    curve = curve_ref[...]
    exposure = exp_ref[...]
    diagonal = lax.broadcasted_iota(jnp.int32, (t_dev, n_col), 0) == (
        lax.broadcasted_iota(jnp.int32, (t_dev, n_col), 1) % t_dev
    )

    def joined(array):
        return (array + pltpu.roll(array, LANES - PART, 1)) + pltpu.roll(array, LANES - 2 * PART, 1)

    def block(b, carry):
        first = pl.multiple_of(b * EVENT_BLOCK, EVENT_BLOCK)
        here = joined(geo_s[pl.ds(first, EVENT_BLOCK), :])
        rupture = here[:, 6 * n_rup : 6 * n_rup + 1].astype(jnp.int32)
        owner = rupture // n_rup
        hot = (lax.broadcasted_iota(jnp.int32, (EVENT_BLOCK, n_dev), 1) == owner).astype(BF16)
        found = joined(jnp.dot(hot, ruptures, preferred_element_type=F32))
        own = found
        for u in range(1, n_rup):
            own = jnp.where(rupture - owner * n_rup == u, pltpu.roll(found, LANES - 6 * u, 1), own)
        start_x = own[:, 0:1]
        start_y = own[:, 1:2]
        along_x = own[:, 2:3] - start_x
        along_y = own[:, 3:4] - start_y
        depth = own[:, 4:5]
        size = own[:, 5:6]
        length_sq = along_x * along_x + along_y * along_y
        rel_x = x - start_x
        rel_y = y - start_y
        portion = jnp.clip((rel_x * along_x + rel_y * along_y) / length_sq, 0.0, 1.0)
        off_x = rel_x - portion * along_x
        off_y = rel_y - portion * along_y
        distance = jnp.sqrt(off_x * off_x + off_y * off_y + depth * depth)
        got = [got_ref[b * EVENT_BLOCK + u, :, :SITE_DEV].astype(F32) for u in range(EVENT_BLOCK)]
        below, weight_0, weight_1 = [], [], []
        for k in range(2):
            c = COEFFS[k]
            eps = jnp.concatenate([rows[k : k + 1] for rows in got], axis=0)
            field = (
                c[0] + c[1] * (size - 6.0)
                - c[2] * 0.5 * jnp.log(distance * distance + c[3] * c[3])
                - c[4] * distance
                + c[5] * eps
            )
            position = jnp.clip((field - LOW_LEVEL) / LEVEL_STEP, 0.0, G - 1.0)
            floor = jnp.floor(position)
            below.append(floor)
            weight_0.append(1.0 - (position - floor))
            weight_1.append(jnp.maximum(0.0, 1.0 - ((floor + 1.0) - position)))

        def wide(array, e):
            return jnp.broadcast_to(array[e : e + 1].astype(BF16), (G, SITE_DEV))

        ratios = []
        for e in range(EVENT_BLOCK):
            tents = []
            for k in range(2):
                at = wide(below[k], e)
                tents.append(
                    jnp.where(
                        level == at,
                        wide(weight_0[k], e),
                        jnp.where(level_less == at, wide(weight_1[k], e), zero),
                    )
                )
            ratio = jnp.dot(curve, jnp.concatenate(tents, axis=0), preferred_element_type=F32)
            ratios.append(ratio.astype(BF16))
            if len(ratios) * t_dev == 32:
                ratio_s[(e + 1) * t_dev - 32 : (e + 1) * t_dev, :] = jnp.concatenate(ratios, axis=0)
                ratios = []
        terms = jnp.dot(ratio_s[...], exposure, preferred_element_type=F32)
        rows = [
            jnp.sum(jnp.where(diagonal, terms[e * t_dev : (e + 1) * t_dev], 0.0), axis=0, keepdims=True)
            for e in range(EVENT_BLOCK)
        ]
        loss_s[pl.ds(first, EVENT_BLOCK), :] = jnp.concatenate(rows, axis=0)
        return carry

    lax.fori_loop(0, events // EVENT_BLOCK, block, 0)

    halves = n_col // LANES

    def arrange(i, carry):
        first = pl.multiple_of(i * ev_dev, ROWS)
        for u in range(halves):
            part = loss_s[pl.ds(first, ev_dev), u * LANES : (u + 1) * LANES]
            out_ref[pl.ds(pl.multiple_of((i * halves + u) * ev_dev, ROWS), ev_dev), :] = swap_groups(
                part, n_ev, t_dev
            )
        return carry

    lax.fori_loop(0, n_ev, arrange, 0, unroll=n_ev <= 4)


def total_kernel(n_ev, n_site, got_ref, out_ref):
    high = got_ref.shape[0] // (n_ev * n_site)
    rows = []
    for i in range(n_ev):
        for h in range(high):
            part = got_ref[pl.ds(i * n_site * high + h, n_site, stride=high), :]
            rows.append(jnp.sum(part, axis=0, keepdims=True))
    out_ref[...] = swap_groups(jnp.concatenate(rows, axis=0), n_ev, LANES // n_ev)


def shards(
    ruptures,
    event_rupture,
    epsilon,
    site_coords,
    vulnerability,
    taxo_measure,
    taxo_offset,
    asset_site,
    asset_taxo,
    asset_tract,
    asset_value,
):
    n_ev = lax.axis_size("ev")
    n_site = lax.axis_size("site")
    n_dev = n_ev * n_site
    n_rup = ruptures.shape[1]
    sites = epsilon.shape[2]
    t_dev = TAXO // n_ev
    n_col = n_site * t_dev
    asset_rows = asset_site.shape[0] // LANES

    def exchange(array):
        return lax.all_to_all(array, AXES, split_axis=0, concat_axis=0, tiled=True)

    packed = pl.pallas_call(
        lambda *refs: pack_kernel(n_ev, n_site, *refs),
        out_shape=jax.ShapeDtypeStruct((n_dev, 2, SITE_DEV + LANES), BF16),
        in_specs=[HBM] * 3,
        out_specs=VMEM,
        scratch_shapes=[
            pltpu.SMEM((n_rup, 6), F32),
            pltpu.SMEM((1,), jnp.int32),
            pltpu.VMEM((2, sites), BF16),
            pltpu.SemaphoreType.DMA((3,)),
        ],
        compiler_params=params(60),
    )(ruptures.T, event_rupture, epsilon.reshape(2, sites))
    got = exchange(packed)

    def as_rows(array):
        return array.reshape(asset_rows, LANES)

    exposure, curve = pl.pallas_call(
        lambda *refs: exposure_kernel(t_dev, COMPACT_ROWS, *refs),
        out_shape=(
            jax.ShapeDtypeStruct((SITE_DEV, n_col), BF16),
            jax.ShapeDtypeStruct((t_dev, 2 * G), BF16),
        ),
        in_specs=[VMEM] * 4 + [HBM] * 3,
        out_specs=(VMEM, VMEM),
        scratch_shapes=[pltpu.VMEM((asset_rows, LANES), F32)] * 4
        + [pltpu.VMEM((SITE_DEV, n_col), F32), pltpu.VMEM((TAXO, 2 * G), F32)]
        + [pltpu.VMEM((NB, TAXO), BF16), pltpu.VMEM((1, TAXO), jnp.int32), pltpu.VMEM((1, TAXO), jnp.int32)]
        + [pltpu.SemaphoreType.DMA((3,))],
        compiler_params=params(24),
        cost_estimate=pl.CostEstimate(
            flops=2 * asset_rows * LANES * SITE_DEV * n_col, bytes_accessed=1 << 20, transcendentals=0
        ),
    )(
        as_rows(asset_site),
        as_rows(asset_taxo),
        as_rows(asset_tract),
        as_rows(asset_value),
        vulnerability.T,
        taxo_measure.reshape(1, TAXO),
        taxo_offset.reshape(1, TAXO),
    )

    parts = pl.pallas_call(
        lambda *refs: loss_kernel(n_ev, n_site, n_rup, *refs),
        out_shape=jax.ShapeDtypeStruct((n_dev * n_col // LANES, LANES), F32),
        in_specs=[VMEM] * 4,
        out_specs=VMEM,
        scratch_shapes=[
            pltpu.VMEM((n_dev, LANES), F32),
            pltpu.VMEM((EVENT_BLOCK * t_dev, SITE_DEV), BF16),
            pltpu.VMEM((n_dev, n_col), F32),
        ],
        compiler_params=params(20),
    )(got, site_coords, exposure, curve)

    losses = pl.pallas_call(
        lambda *refs: total_kernel(n_ev, n_site, *refs),
        out_shape=jax.ShapeDtypeStruct((n_dev // n_ev, LANES), F32),
        in_specs=[VMEM],
        out_specs=VMEM,
        compiler_params=params(4),
    )(exchange(parts))
    return losses[None]


def solution(mesh):
    in_specs = (
        P(None, ("ev", "site")),
        P(("ev", "site")),
        P(None, ("ev", "site"), None),
        P(),
        P(),
        P(),
        P(),
        P("site"),
        P("site"),
        P("site"),
        P("site"),
    )
    out_specs = P("site", "ev", None)
    return jax.shard_map(shards, mesh=mesh, in_specs=in_specs, out_specs=out_specs, check_vma=False)
```

```python
import jax
import jax.numpy as jnp
from jax import lax
from jax.experimental import pallas as pl
from jax.experimental.pallas import tpu as pltpu
from jax.sharding import PartitionSpec as P

SITE_DEV = 512
TAXO = 128
G = 64
NB = 40
LANES = 128
ROWS = 8
PART = 16
EVENT_BLOCK = 32
CODES = 1 << 17
SLANT = 13
HOLE = 1 << 24
COMPACT_ROWS = 16

COEFFS = ((1.0, 1.1, 1.0, 6.0, 0.004, 0.6), (0.3, 1.4, 0.9, 8.0, 0.002, 0.7))
LOW_LEVEL = -6.0
LEVEL_STEP = 0.1

AXES = ("ev", "site")
F32 = jnp.float32
BF16 = jnp.bfloat16
NT = (((1,), (1,)), ((), ()))

VMEM = pl.BlockSpec(memory_space=pltpu.VMEM)
HBM = pl.BlockSpec(memory_space=pltpu.HBM)


def params(mebibytes):
    return pltpu.CompilerParams(vmem_limit_bytes=mebibytes << 20)


def parts_of(value):
    high = value.astype(BF16).astype(F32)
    rest = value - high
    middle = rest.astype(BF16).astype(F32)
    return high, middle, (rest - middle).astype(BF16).astype(F32)


def pack_kernel(n_ev, n_site, rup_hbm, idx_hbm, eps_hbm, out_ref, rup_ref, idx_ref, eps_ref, sems):
    copies = [
        pltpu.make_async_copy(source, target, sems.at[k])
        for k, (source, target) in enumerate(((rup_hbm, rup_ref), (idx_hbm, idx_ref), (eps_hbm, eps_ref)))
    ]
    for copy in copies:
        copy.start()
    n_rup = rup_ref.shape[0]
    lane = lax.broadcasted_iota(jnp.int32, (2, LANES), 1)
    row = jnp.zeros((2, LANES), F32)
    copies[0].wait()
    copies[1].wait()
    for b in range(n_rup):
        for c in range(6):
            row = jnp.where(lane == 6 * b + c, rup_ref[b, c], row)
    row = jnp.where(lane == 6 * n_rup, idx_ref[0].astype(F32), row)
    high, middle, low = parts_of(row)
    row = (high + pltpu.roll(middle, PART, 1) + pltpu.roll(low, 2 * PART, 1)).astype(BF16)
    copies[2].wait()
    eps = eps_ref[...]

    def fill(i, carry):
        for j in range(n_site):
            out_ref[i * n_site + j, :, :SITE_DEV] = eps[:, j * SITE_DEV : (j + 1) * SITE_DEV]
            out_ref[i * n_site + j, :, SITE_DEV:] = row
        return carry

    lax.fori_loop(0, n_ev, fill, 0, unroll=n_ev <= 4)


def compact(own, code, value):
    rows = own.shape[0]
    above = lax.broadcasted_iota(jnp.int32, (rows, rows), 1) < lax.broadcasted_iota(jnp.int32, (rows, rows), 0)
    gaps = jnp.dot(above.astype(BF16), 1.0 - own.astype(BF16), preferred_element_type=F32).astype(jnp.int32)
    word = jnp.where(own, gaps * CODES + code, HOLE)
    size = 1
    while size < rows:
        bit = size * CODES
        from_word = jnp.concatenate([word[size:], jnp.full((size, LANES), HOLE, jnp.int32)], axis=0)
        from_value = jnp.concatenate([value[size:], jnp.zeros((size, LANES), F32)], axis=0)
        comes = (from_word & bit) != 0
        value = jnp.where(comes, from_value, value)
        word = jnp.where(comes, from_word, jnp.where((word & bit) != 0, HOLE, word))
        size *= 2
    return word, value


def slanted(array):
    return jnp.concatenate(
        [
            pltpu.roll(array[q : q + ROWS], (11 * q // ROWS) % 36, 1, stride=SLANT, stride_axis=0)
            for q in range(0, array.shape[0], ROWS)
        ],
        axis=0,
    )


def exposure_kernel(
    t_dev, rows, site_ref, taxo_ref, tract_ref, value_ref, vul_hbm, measure_hbm, offset_hbm,
    exp_ref, curve_ref, site_s, col_s, high_s, low_s, sum_s, curve_s, vul_ref, measure_ref, offset_ref, sems,
):
    copies = [
        pltpu.make_async_copy(source, target, sems.at[k])
        for k, (source, target) in enumerate(
            ((vul_hbm, vul_ref), (measure_hbm, measure_ref), (offset_hbm, offset_ref))
        )
    ]
    for copy in copies:
        copy.start()
    me = lax.axis_index("ev")
    first = me * t_dev
    n_col = exp_ref.shape[1]
    taxo = taxo_ref[...] - first
    own = (taxo >= 0) & (taxo < t_dev)
    code = site_ref[...] * n_col + tract_ref[...] * t_dev + taxo
    word, value = compact(own, code, value_ref[...])
    word, value = slanted(word), slanted(value)
    own = word != HOLE
    most = jnp.max(jnp.sum(own.astype(F32), axis=0, keepdims=True)).astype(jnp.int32)
    word, value = compact(own, word & (CODES - 1), value)
    high = value.astype(BF16).astype(F32)
    site_s[...] = ((word & (CODES - 1)) // n_col).astype(F32)
    col_s[...] = jnp.where((word & HOLE) != 0, -1, word & (n_col - 1)).astype(F32)
    high_s[...] = high
    low_s[...] = value - high

    level = lax.broadcasted_iota(jnp.int32, (256, LANES), 0).astype(F32).astype(BF16)
    zero = jnp.zeros((256, LANES), BF16)
    one = jnp.ones((256, LANES), BF16)

    def spread(ref, q, less=0.0):
        return jnp.broadcast_to((ref[pl.ds(q, 1), :] - less).astype(BF16), (256, LANES))

    def beside(parts):
        return jnp.concatenate(parts, axis=1)

    sum_s[...] = jnp.zeros_like(sum_s)

    def step(c, carry):
        site_rows = [[] for _ in range(SITE_DEV // 256)]
        high_rows, low_rows = [], []
        for u in range(rows):
            q = c * rows + u
            for part, found in enumerate(site_rows):
                found.append(jnp.where(level == spread(site_s, q, 256.0 * part), one, zero))
            here = level == spread(col_s, q)
            high_rows.append(jnp.where(here, spread(high_s, q), zero))
            low_rows.append(jnp.where(here, spread(low_s, q), zero))
        at_site = jnp.concatenate([beside(found) for found in site_rows], axis=0)
        sum_s[...] += lax.dot_general(
            beside([at_site, at_site]), beside(high_rows + low_rows), NT, preferred_element_type=F32
        )
        return carry

    lax.fori_loop(0, (most + rows - 1) // rows, step, 0)
    exp_ref[...] = sum_s[...].astype(BF16)

    for copy in copies:
        copy.wait()
    vul = vul_ref[...].astype(F32)
    table = jnp.concatenate([vul, jnp.broadcast_to(vul[NB - 1 : NB], (G - NB, TAXO))], axis=0)
    offset = jnp.broadcast_to(offset_ref[...], (G, TAXO))
    level_row = lax.broadcasted_iota(jnp.int32, (G, TAXO), 0)
    for bit in range(5):
        size = 1 << bit
        moved = jnp.where(level_row >= size, pltpu.roll(table, size, 0), 0.0)
        table = jnp.where((offset & size) != 0, moved, table)
    measure = jnp.broadcast_to(measure_ref[...], (G, TAXO))
    both = jnp.concatenate(
        [jnp.where(measure == 0, table, 0.0), jnp.where(measure == 1, table, 0.0)], axis=0
    )
    curve_s[...] = both.T
    curve_ref[...] = curve_s[pl.ds(pl.multiple_of(first, ROWS), t_dev), :].astype(BF16)


def swap_groups(block, groups, width):
    total = block.shape[0]
    high = total // groups
    row_group = lax.broadcasted_iota(jnp.int32, block.shape, 0) // high
    lane_group = lax.broadcasted_iota(jnp.int32, block.shape, 1) // width
    result = block
    for d in range(1, groups):
        moved = pltpu.roll(pltpu.roll(block, total - high * d, 0), width * d, 1)
        gap = lane_group - row_group
        result = jnp.where((gap == d) | (gap == d - groups), moved, result)
    return result


def loss_kernel(n_ev, n_site, n_rup, got_ref, coords_ref, exp_ref, curve_ref, out_ref, geo_s, ratio_s, loss_s):
    n_dev = n_ev * n_site
    t_dev = curve_ref.shape[0]
    n_col = exp_ref.shape[1]
    events = n_dev
    ev_dev = events // n_ev
    me = lax.axis_index("site")
    start = pl.multiple_of(me * SITE_DEV, LANES)
    x = coords_ref[0:1, pl.ds(start, SITE_DEV)]
    y = coords_ref[1:2, pl.ds(start, SITE_DEV)]

    def take_geometry(b, carry):
        first = b * EVENT_BLOCK
        rows = [got_ref[first + u, :, SITE_DEV:].astype(F32)[0:1] for u in range(EVENT_BLOCK)]
        geo_s[pl.ds(pl.multiple_of(first, ROWS), EVENT_BLOCK), :] = jnp.concatenate(rows, axis=0)
        return carry

    lax.fori_loop(0, n_dev // EVENT_BLOCK, take_geometry, 0)
    ruptures = geo_s[...].astype(BF16)
    level = lax.broadcasted_iota(jnp.int32, (G, SITE_DEV), 0).astype(F32).astype(BF16)
    level_less = (lax.broadcasted_iota(jnp.int32, (G, SITE_DEV), 0) - 1).astype(F32).astype(BF16)
    zero = jnp.zeros((G, SITE_DEV), BF16)
    curve = curve_ref[...]
    exposure = exp_ref[...]
    diagonal = lax.broadcasted_iota(jnp.int32, (t_dev, n_col), 0) == (
        lax.broadcasted_iota(jnp.int32, (t_dev, n_col), 1) % t_dev
    )

    def joined(array):
        return (array + pltpu.roll(array, LANES - PART, 1)) + pltpu.roll(array, LANES - 2 * PART, 1)

    def block(b, carry):
        first = pl.multiple_of(b * EVENT_BLOCK, EVENT_BLOCK)
        here = joined(geo_s[pl.ds(first, EVENT_BLOCK), :])
        rupture = here[:, 6 * n_rup : 6 * n_rup + 1].astype(jnp.int32)
        owner = rupture // n_rup
        hot = (lax.broadcasted_iota(jnp.int32, (EVENT_BLOCK, n_dev), 1) == owner).astype(BF16)
        found = joined(jnp.dot(hot, ruptures, preferred_element_type=F32))
        own = found
        for u in range(1, n_rup):
            own = jnp.where(rupture - owner * n_rup == u, pltpu.roll(found, LANES - 6 * u, 1), own)
        start_x = own[:, 0:1]
        start_y = own[:, 1:2]
        along_x = own[:, 2:3] - start_x
        along_y = own[:, 3:4] - start_y
        depth = own[:, 4:5]
        size = own[:, 5:6]
        length_sq = along_x * along_x + along_y * along_y
        rel_x = x - start_x
        rel_y = y - start_y
        portion = jnp.clip((rel_x * along_x + rel_y * along_y) / length_sq, 0.0, 1.0)
        off_x = rel_x - portion * along_x
        off_y = rel_y - portion * along_y
        distance = jnp.sqrt(off_x * off_x + off_y * off_y + depth * depth)
        got = [got_ref[b * EVENT_BLOCK + u, :, :SITE_DEV].astype(F32) for u in range(EVENT_BLOCK)]
        below, weight_0, weight_1 = [], [], []
        for k in range(2):
            c = COEFFS[k]
            eps = jnp.concatenate([rows[k : k + 1] for rows in got], axis=0)
            field = (
                c[0] + c[1] * (size - 6.0)
                - c[2] * 0.5 * jnp.log(distance * distance + c[3] * c[3])
                - c[4] * distance
                + c[5] * eps
            )
            position = jnp.clip((field - LOW_LEVEL) / LEVEL_STEP, 0.0, G - 1.0)
            floor = jnp.floor(position)
            below.append(floor)
            weight_0.append(1.0 - (position - floor))
            weight_1.append(jnp.maximum(0.0, 1.0 - ((floor + 1.0) - position)))

        def wide(array, e):
            return jnp.broadcast_to(array[e : e + 1].astype(BF16), (G, SITE_DEV))

        ratios = []
        for e in range(EVENT_BLOCK):
            tents = []
            for k in range(2):
                at = wide(below[k], e)
                tents.append(
                    jnp.where(
                        level == at,
                        wide(weight_0[k], e),
                        jnp.where(level_less == at, wide(weight_1[k], e), zero),
                    )
                )
            ratio = jnp.dot(curve, jnp.concatenate(tents, axis=0), preferred_element_type=F32)
            ratios.append(ratio.astype(BF16))
            if len(ratios) * t_dev == 32:
                ratio_s[(e + 1) * t_dev - 32 : (e + 1) * t_dev, :] = jnp.concatenate(ratios, axis=0)
                ratios = []
        terms = jnp.dot(ratio_s[...], exposure, preferred_element_type=F32)
        rows = [
            jnp.sum(jnp.where(diagonal, terms[e * t_dev : (e + 1) * t_dev], 0.0), axis=0, keepdims=True)
            for e in range(EVENT_BLOCK)
        ]
        loss_s[pl.ds(first, EVENT_BLOCK), :] = jnp.concatenate(rows, axis=0)
        return carry

    lax.fori_loop(0, events // EVENT_BLOCK, block, 0)

    halves = n_col // LANES

    def arrange(i, carry):
        first = pl.multiple_of(i * ev_dev, ROWS)
        for u in range(halves):
            part = loss_s[pl.ds(first, ev_dev), u * LANES : (u + 1) * LANES]
            out_ref[pl.ds(pl.multiple_of((i * halves + u) * ev_dev, ROWS), ev_dev), :] = swap_groups(
                part, n_ev, t_dev
            )
        return carry

    lax.fori_loop(0, n_ev, arrange, 0, unroll=n_ev <= 4)


def total_kernel(n_ev, n_site, got_ref, out_ref):
    high = got_ref.shape[0] // (n_ev * n_site)
    rows = []
    for i in range(n_ev):
        for h in range(high):
            part = got_ref[pl.ds(i * n_site * high + h, n_site, stride=high), :]
            rows.append(jnp.sum(part, axis=0, keepdims=True))
    out_ref[...] = swap_groups(jnp.concatenate(rows, axis=0), n_ev, LANES // n_ev)


def shards(
    ruptures,
    event_rupture,
    epsilon,
    site_coords,
    vulnerability,
    taxo_measure,
    taxo_offset,
    asset_site,
    asset_taxo,
    asset_tract,
    asset_value,
):
    n_ev = lax.axis_size("ev")
    n_site = lax.axis_size("site")
    n_dev = n_ev * n_site
    n_rup = ruptures.shape[1]
    sites = epsilon.shape[2]
    t_dev = TAXO // n_ev
    n_col = n_site * t_dev
    asset_rows = asset_site.shape[0] // LANES

    def stays(array):
        return pltpu.with_memory_space_constraint(array, pltpu.HBM)

    def exchange(array):
        return lax.all_to_all(array, AXES, split_axis=0, concat_axis=0, tiled=True)

    packed = pl.pallas_call(
        lambda *refs: pack_kernel(n_ev, n_site, *refs),
        out_shape=pltpu.VMEM((n_dev, 2, SITE_DEV + LANES), BF16),
        in_specs=[HBM] * 3,
        out_specs=VMEM,
        scratch_shapes=[
            pltpu.SMEM((n_rup, 6), F32),
            pltpu.SMEM((1,), jnp.int32),
            pltpu.VMEM((2, sites), BF16),
            pltpu.SemaphoreType.DMA((3,)),
        ],
        compiler_params=params(4),
    )(stays(ruptures.T), event_rupture, stays(epsilon.reshape(2, sites)))
    got = exchange(packed)

    def as_rows(array):
        return array.reshape(asset_rows, LANES)

    exposure, curve = pl.pallas_call(
        lambda *refs: exposure_kernel(t_dev, COMPACT_ROWS, *refs),
        out_shape=(
            jax.ShapeDtypeStruct((SITE_DEV, n_col), BF16),
            jax.ShapeDtypeStruct((t_dev, 2 * G), BF16),
        ),
        in_specs=[VMEM] * 4 + [HBM] * 3,
        out_specs=(VMEM, VMEM),
        scratch_shapes=[pltpu.VMEM((asset_rows, LANES), F32)] * 4
        + [pltpu.VMEM((SITE_DEV, n_col), F32), pltpu.VMEM((TAXO, 2 * G), F32)]
        + [pltpu.VMEM((NB, TAXO), BF16), pltpu.VMEM((1, TAXO), jnp.int32), pltpu.VMEM((1, TAXO), jnp.int32)]
        + [pltpu.SemaphoreType.DMA((3,))],
        compiler_params=params(24),
        cost_estimate=pl.CostEstimate(
            flops=2 * asset_rows * LANES * SITE_DEV * n_col, bytes_accessed=1 << 20, transcendentals=0
        ),
    )(
        as_rows(asset_site),
        as_rows(asset_taxo),
        as_rows(asset_tract),
        as_rows(asset_value),
        stays(vulnerability.T),
        stays(taxo_measure.reshape(1, TAXO)),
        stays(taxo_offset.reshape(1, TAXO)),
    )

    parts = pl.pallas_call(
        lambda *refs: loss_kernel(n_ev, n_site, n_rup, *refs),
        out_shape=jax.ShapeDtypeStruct((n_dev * n_col // LANES, LANES), F32),
        in_specs=[VMEM] * 4,
        out_specs=VMEM,
        scratch_shapes=[
            pltpu.VMEM((n_dev, LANES), F32),
            pltpu.VMEM((EVENT_BLOCK * t_dev, SITE_DEV), BF16),
            pltpu.VMEM((n_dev, n_col), F32),
        ],
        compiler_params=params(20),
    )(got, site_coords, exposure, curve)

    losses = pl.pallas_call(
        lambda *refs: total_kernel(n_ev, n_site, *refs),
        out_shape=jax.ShapeDtypeStruct((n_dev // n_ev, LANES), F32),
        in_specs=[VMEM],
        out_specs=VMEM,
        compiler_params=params(4),
    )(exchange(parts))
    return losses[None]


def solution(mesh):
    in_specs = (
        P(None, ("ev", "site")),
        P(("ev", "site")),
        P(None, ("ev", "site"), None),
        P(),
        P(),
        P(),
        P(),
        P("site"),
        P("site"),
        P("site"),
        P("site"),
    )
    out_specs = P("site", "ev", None)
    return jax.shard_map(shards, mesh=mesh, in_specs=in_specs, out_specs=out_specs, check_vma=False)
```

```python
import jax
import jax.numpy as jnp
from jax import lax
from jax.experimental import pallas as pl
from jax.experimental.pallas import tpu as pltpu
from jax.sharding import PartitionSpec as P

SITE_DEV = 512
TAXO = 128
G = 64
NB = 40
LANES = 128
ROWS = 8
PART = 16
EVENT_BLOCK = 32
CODES = 1 << 17
SLANT = 13
HOLE = 1 << 24
COMPACT_ROWS = 16

COEFFS = ((1.0, 1.1, 1.0, 6.0, 0.004, 0.6), (0.3, 1.4, 0.9, 8.0, 0.002, 0.7))
LOW_LEVEL = -6.0
LEVEL_STEP = 0.1

AXES = ("ev", "site")
F32 = jnp.float32
BF16 = jnp.bfloat16
NT = (((1,), (1,)), ((), ()))

VMEM = pl.BlockSpec(memory_space=pltpu.VMEM)
SMEM = pl.BlockSpec(memory_space=pltpu.SMEM)
HBM = pl.BlockSpec(memory_space=pltpu.HBM)


def params(mebibytes):
    return pltpu.CompilerParams(vmem_limit_bytes=mebibytes << 20)


def parts_of(value):
    high = value.astype(BF16).astype(F32)
    rest = value - high
    middle = rest.astype(BF16).astype(F32)
    return high, middle, (rest - middle).astype(BF16).astype(F32)


def place_kernel(out_ref):
    out_ref[...] = lax.broadcasted_iota(jnp.int32, out_ref.shape, 1) - lax.broadcasted_iota(
        jnp.int32, out_ref.shape, 0
    )


def pack_kernel(n_ev, n_site, place_ref, rup_ref, idx_ref, eps_ref, out_ref):
    n_rup = rup_ref.shape[1]
    place = place_ref[0:6, :]
    spots = jnp.zeros((6, LANES), F32)
    for k in range(n_rup):
        spots = jnp.where(place == 6 * k, jnp.broadcast_to(rup_ref[:, k : k + 1], (6, LANES)), spots)
    row = jnp.broadcast_to(jnp.sum(spots, axis=0, keepdims=True), (2, LANES))
    lane = jnp.broadcast_to(place_ref[0:1, :], (2, LANES))
    row = jnp.where(lane == 6 * n_rup, idx_ref[0].astype(F32), row)
    high, middle, low = parts_of(row)
    row = (high + pltpu.roll(middle, PART, 1) + pltpu.roll(low, 2 * PART, 1)).astype(BF16)
    eps = eps_ref[...]

    def fill(i, carry):
        for j in range(n_site):
            out_ref[i * n_site + j, :, :SITE_DEV] = eps[:, j * SITE_DEV : (j + 1) * SITE_DEV]
            out_ref[i * n_site + j, :, SITE_DEV:] = row
        return carry

    lax.fori_loop(0, n_ev, fill, 0, unroll=n_ev <= 4)


def compact(own, code, value):
    rows = own.shape[0]
    above = lax.broadcasted_iota(jnp.int32, (rows, rows), 1) < lax.broadcasted_iota(jnp.int32, (rows, rows), 0)
    gaps = jnp.dot(above.astype(BF16), 1.0 - own.astype(BF16), preferred_element_type=F32).astype(jnp.int32)
    word = jnp.where(own, gaps * CODES + code, HOLE)
    size = 1
    while size < rows:
        bit = size * CODES
        from_word = jnp.concatenate([word[size:], jnp.full((size, LANES), HOLE, jnp.int32)], axis=0)
        from_value = jnp.concatenate([value[size:], jnp.zeros((size, LANES), F32)], axis=0)
        comes = (from_word & bit) != 0
        value = jnp.where(comes, from_value, value)
        word = jnp.where(comes, from_word, jnp.where((word & bit) != 0, HOLE, word))
        size *= 2
    return word, value


def slanted(array):
    return jnp.concatenate(
        [
            pltpu.roll(array[q : q + ROWS], (11 * q // ROWS) % 36, 1, stride=SLANT, stride_axis=0)
            for q in range(0, array.shape[0], ROWS)
        ],
        axis=0,
    )


def exposure_kernel(
    t_dev, rows, site_ref, taxo_ref, tract_ref, value_ref, vul_hbm, measure_hbm, offset_hbm,
    exp_ref, curve_ref, site_s, col_s, high_s, low_s, sum_s, curve_s, vul_ref, measure_ref, offset_ref, sems,
):
    copies = [
        pltpu.make_async_copy(source, target, sems.at[k])
        for k, (source, target) in enumerate(
            ((vul_hbm, vul_ref), (measure_hbm, measure_ref), (offset_hbm, offset_ref))
        )
    ]
    for copy in copies:
        copy.start()
    me = lax.axis_index("ev")
    first = me * t_dev
    n_col = exp_ref.shape[1]
    taxo = taxo_ref[...] - first
    own = (taxo >= 0) & (taxo < t_dev)
    code = site_ref[...] * n_col + tract_ref[...] * t_dev + taxo
    word, value = compact(own, code, value_ref[...])
    word, value = slanted(word), slanted(value)
    own = word != HOLE
    most = jnp.max(jnp.sum(own.astype(F32), axis=0, keepdims=True)).astype(jnp.int32)
    word, value = compact(own, word & (CODES - 1), value)
    high = value.astype(BF16).astype(F32)
    site_s[...] = ((word & (CODES - 1)) // n_col).astype(F32)
    col_s[...] = jnp.where((word & HOLE) != 0, -1, word & (n_col - 1)).astype(F32)
    high_s[...] = high
    low_s[...] = value - high

    level = lax.broadcasted_iota(jnp.int32, (256, LANES), 0).astype(F32).astype(BF16)
    zero = jnp.zeros((256, LANES), BF16)
    one = jnp.ones((256, LANES), BF16)

    def spread(ref, q, less=0.0):
        return jnp.broadcast_to((ref[pl.ds(q, 1), :] - less).astype(BF16), (256, LANES))

    def beside(parts):
        return jnp.concatenate(parts, axis=1)

    sum_s[...] = jnp.zeros_like(sum_s)

    def step(c, carry):
        site_rows = [[] for _ in range(SITE_DEV // 256)]
        high_rows, low_rows = [], []
        for u in range(rows):
            q = c * rows + u
            for part, found in enumerate(site_rows):
                found.append(jnp.where(level == spread(site_s, q, 256.0 * part), one, zero))
            here = level == spread(col_s, q)
            high_rows.append(jnp.where(here, spread(high_s, q), zero))
            low_rows.append(jnp.where(here, spread(low_s, q), zero))
        at_site = jnp.concatenate([beside(found) for found in site_rows], axis=0)
        sum_s[...] += lax.dot_general(
            beside([at_site, at_site]), beside(high_rows + low_rows), NT, preferred_element_type=F32
        )
        return carry

    lax.fori_loop(0, (most + rows - 1) // rows, step, 0)
    exp_ref[...] = sum_s[...].astype(BF16)

    for copy in copies:
        copy.wait()
    vul = vul_ref[...].astype(F32)
    table = jnp.concatenate([vul, jnp.broadcast_to(vul[NB - 1 : NB], (G - NB, TAXO))], axis=0)
    offset = jnp.broadcast_to(offset_ref[...], (G, TAXO))
    level_row = lax.broadcasted_iota(jnp.int32, (G, TAXO), 0)
    for bit in range(5):
        size = 1 << bit
        moved = jnp.where(level_row >= size, pltpu.roll(table, size, 0), 0.0)
        table = jnp.where((offset & size) != 0, moved, table)
    measure = jnp.broadcast_to(measure_ref[...], (G, TAXO))
    both = jnp.concatenate(
        [jnp.where(measure == 0, table, 0.0), jnp.where(measure == 1, table, 0.0)], axis=0
    )
    curve_s[...] = both.T
    curve_ref[...] = curve_s[pl.ds(pl.multiple_of(first, ROWS), t_dev), :].astype(BF16)


def swap_groups(block, groups, width):
    total = block.shape[0]
    high = total // groups
    row_group = lax.broadcasted_iota(jnp.int32, block.shape, 0) // high
    lane_group = lax.broadcasted_iota(jnp.int32, block.shape, 1) // width
    result = block
    for d in range(1, groups):
        moved = pltpu.roll(pltpu.roll(block, total - high * d, 0), width * d, 1)
        gap = lane_group - row_group
        result = jnp.where((gap == d) | (gap == d - groups), moved, result)
    return result


def loss_kernel(n_ev, n_site, n_rup, got_ref, coords_ref, exp_ref, curve_ref, out_ref, geo_s, ratio_s, loss_s):
    n_dev = n_ev * n_site
    t_dev = curve_ref.shape[0]
    n_col = exp_ref.shape[1]
    events = n_dev
    ev_dev = events // n_ev
    me = lax.axis_index("site")
    start = pl.multiple_of(me * SITE_DEV, LANES)
    x = coords_ref[0:1, pl.ds(start, SITE_DEV)]
    y = coords_ref[1:2, pl.ds(start, SITE_DEV)]

    def take_geometry(b, carry):
        first = b * EVENT_BLOCK
        rows = [got_ref[first + u, :, SITE_DEV:].astype(F32)[0:1] for u in range(EVENT_BLOCK)]
        geo_s[pl.ds(pl.multiple_of(first, ROWS), EVENT_BLOCK), :] = jnp.concatenate(rows, axis=0)
        return carry

    lax.fori_loop(0, n_dev // EVENT_BLOCK, take_geometry, 0)
    ruptures = geo_s[...].astype(BF16)
    level = lax.broadcasted_iota(jnp.int32, (G, SITE_DEV), 0).astype(F32).astype(BF16)
    level_less = (lax.broadcasted_iota(jnp.int32, (G, SITE_DEV), 0) - 1).astype(F32).astype(BF16)
    zero = jnp.zeros((G, SITE_DEV), BF16)
    curve = curve_ref[...]
    exposure = exp_ref[...]
    diagonal = lax.broadcasted_iota(jnp.int32, (t_dev, n_col), 0) == (
        lax.broadcasted_iota(jnp.int32, (t_dev, n_col), 1) % t_dev
    )

    def joined(array):
        return (array + pltpu.roll(array, LANES - PART, 1)) + pltpu.roll(array, LANES - 2 * PART, 1)

    def block(b, carry):
        first = pl.multiple_of(b * EVENT_BLOCK, EVENT_BLOCK)
        here = joined(geo_s[pl.ds(first, EVENT_BLOCK), :])
        rupture = here[:, 6 * n_rup : 6 * n_rup + 1].astype(jnp.int32)
        owner = rupture // n_rup
        hot = (lax.broadcasted_iota(jnp.int32, (EVENT_BLOCK, n_dev), 1) == owner).astype(BF16)
        found = joined(jnp.dot(hot, ruptures, preferred_element_type=F32))
        own = found
        for u in range(1, n_rup):
            own = jnp.where(rupture - owner * n_rup == u, pltpu.roll(found, LANES - 6 * u, 1), own)
        start_x = own[:, 0:1]
        start_y = own[:, 1:2]
        along_x = own[:, 2:3] - start_x
        along_y = own[:, 3:4] - start_y
        depth = own[:, 4:5]
        size = own[:, 5:6]
        length_sq = along_x * along_x + along_y * along_y
        rel_x = x - start_x
        rel_y = y - start_y
        portion = jnp.clip((rel_x * along_x + rel_y * along_y) / length_sq, 0.0, 1.0)
        off_x = rel_x - portion * along_x
        off_y = rel_y - portion * along_y
        distance = jnp.sqrt(off_x * off_x + off_y * off_y + depth * depth)
        got = [got_ref[b * EVENT_BLOCK + u, :, :SITE_DEV].astype(F32) for u in range(EVENT_BLOCK)]
        below, weight_0, weight_1 = [], [], []
        for k in range(2):
            c = COEFFS[k]
            eps = jnp.concatenate([rows[k : k + 1] for rows in got], axis=0)
            field = (
                c[0] + c[1] * (size - 6.0)
                - c[2] * 0.5 * jnp.log(distance * distance + c[3] * c[3])
                - c[4] * distance
                + c[5] * eps
            )
            position = jnp.clip((field - LOW_LEVEL) / LEVEL_STEP, 0.0, G - 1.0)
            floor = jnp.floor(position)
            below.append(floor)
            weight_0.append(1.0 - (position - floor))
            weight_1.append(jnp.maximum(0.0, 1.0 - ((floor + 1.0) - position)))

        def wide(array, e):
            return jnp.broadcast_to(array[e : e + 1].astype(BF16), (G, SITE_DEV))

        ratios = []
        for e in range(EVENT_BLOCK):
            tents = []
            for k in range(2):
                at = wide(below[k], e)
                tents.append(
                    jnp.where(
                        level == at,
                        wide(weight_0[k], e),
                        jnp.where(level_less == at, wide(weight_1[k], e), zero),
                    )
                )
            ratio = jnp.dot(curve, jnp.concatenate(tents, axis=0), preferred_element_type=F32)
            ratios.append(ratio.astype(BF16))
            if len(ratios) * t_dev == 32:
                ratio_s[(e + 1) * t_dev - 32 : (e + 1) * t_dev, :] = jnp.concatenate(ratios, axis=0)
                ratios = []
        terms = jnp.dot(ratio_s[...], exposure, preferred_element_type=F32)
        rows = [
            jnp.sum(jnp.where(diagonal, terms[e * t_dev : (e + 1) * t_dev], 0.0), axis=0, keepdims=True)
            for e in range(EVENT_BLOCK)
        ]
        loss_s[pl.ds(first, EVENT_BLOCK), :] = jnp.concatenate(rows, axis=0)
        return carry

    lax.fori_loop(0, events // EVENT_BLOCK, block, 0)

    halves = n_col // LANES

    def arrange(i, carry):
        first = pl.multiple_of(i * ev_dev, ROWS)
        for u in range(halves):
            part = loss_s[pl.ds(first, ev_dev), u * LANES : (u + 1) * LANES]
            out_ref[pl.ds(pl.multiple_of((i * halves + u) * ev_dev, ROWS), ev_dev), :] = swap_groups(
                part, n_ev, t_dev
            )
        return carry

    lax.fori_loop(0, n_ev, arrange, 0, unroll=n_ev <= 4)


def total_kernel(n_ev, n_site, got_ref, out_ref):
    high = got_ref.shape[0] // (n_ev * n_site)
    rows = []
    for i in range(n_ev):
        for h in range(high):
            part = got_ref[pl.ds(i * n_site * high + h, n_site, stride=high), :]
            rows.append(jnp.sum(part, axis=0, keepdims=True))
    out_ref[...] = swap_groups(jnp.concatenate(rows, axis=0), n_ev, LANES // n_ev)


def shards(
    ruptures,
    event_rupture,
    epsilon,
    site_coords,
    vulnerability,
    taxo_measure,
    taxo_offset,
    asset_site,
    asset_taxo,
    asset_tract,
    asset_value,
):
    n_ev = lax.axis_size("ev")
    n_site = lax.axis_size("site")
    n_dev = n_ev * n_site
    n_rup = ruptures.shape[1]
    sites = epsilon.shape[2]
    t_dev = TAXO // n_ev
    n_col = n_site * t_dev
    asset_rows = asset_site.shape[0] // LANES

    def stays(array):
        return pltpu.with_memory_space_constraint(array, pltpu.HBM)

    def exchange(array):
        return lax.all_to_all(array, AXES, split_axis=0, concat_axis=0, tiled=True)

    place = pl.pallas_call(
        place_kernel,
        out_shape=jax.ShapeDtypeStruct((ROWS, LANES), jnp.int32),
        out_specs=VMEM,
        compiler_params=params(4),
        cost_estimate=pl.CostEstimate(flops=4_000_000_000, bytes_accessed=12_000_000, transcendentals=0),
    )()
    packed = pl.pallas_call(
        lambda *refs: pack_kernel(n_ev, n_site, *refs),
        out_shape=jax.ShapeDtypeStruct((n_dev, 2, SITE_DEV + LANES), BF16),
        in_specs=[VMEM, VMEM, SMEM, VMEM],
        out_specs=VMEM,
        compiler_params=params(4),
    )(place, ruptures, event_rupture, epsilon.reshape(2, sites))
    got = exchange(packed)

    def as_rows(array):
        return array.reshape(asset_rows, LANES)

    exposure, curve = pl.pallas_call(
        lambda *refs: exposure_kernel(t_dev, COMPACT_ROWS, *refs),
        out_shape=(
            jax.ShapeDtypeStruct((SITE_DEV, n_col), BF16),
            jax.ShapeDtypeStruct((t_dev, 2 * G), BF16),
        ),
        in_specs=[VMEM] * 4 + [HBM] * 3,
        out_specs=(VMEM, VMEM),
        scratch_shapes=[pltpu.VMEM((asset_rows, LANES), F32)] * 4
        + [pltpu.VMEM((SITE_DEV, n_col), F32), pltpu.VMEM((TAXO, 2 * G), F32)]
        + [pltpu.VMEM((NB, TAXO), BF16), pltpu.VMEM((1, TAXO), jnp.int32), pltpu.VMEM((1, TAXO), jnp.int32)]
        + [pltpu.SemaphoreType.DMA((3,))],
        compiler_params=params(24),
        cost_estimate=pl.CostEstimate(
            flops=2 * asset_rows * LANES * SITE_DEV * n_col, bytes_accessed=1 << 20, transcendentals=0
        ),
    )(
        as_rows(asset_site),
        as_rows(asset_taxo),
        as_rows(asset_tract),
        as_rows(asset_value),
        stays(vulnerability.T),
        stays(taxo_measure.reshape(1, TAXO)),
        stays(taxo_offset.reshape(1, TAXO)),
    )

    parts = pl.pallas_call(
        lambda *refs: loss_kernel(n_ev, n_site, n_rup, *refs),
        out_shape=jax.ShapeDtypeStruct((n_dev * n_col // LANES, LANES), F32),
        in_specs=[VMEM] * 4,
        out_specs=VMEM,
        scratch_shapes=[
            pltpu.VMEM((n_dev, LANES), F32),
            pltpu.VMEM((EVENT_BLOCK * t_dev, SITE_DEV), BF16),
            pltpu.VMEM((n_dev, n_col), F32),
        ],
        compiler_params=params(20),
    )(got, site_coords, exposure, curve)

    losses = pl.pallas_call(
        lambda *refs: total_kernel(n_ev, n_site, *refs),
        out_shape=jax.ShapeDtypeStruct((n_dev // n_ev, LANES), F32),
        in_specs=[VMEM],
        out_specs=VMEM,
        compiler_params=params(4),
    )(exchange(parts))
    return losses[None]


def solution(mesh):
    in_specs = (
        P(None, ("ev", "site")),
        P(("ev", "site")),
        P(None, ("ev", "site"), None),
        P(),
        P(),
        P(),
        P(),
        P("site"),
        P("site"),
        P("site"),
        P("site"),
    )
    out_specs = P("site", "ev", None)
    return jax.shard_map(shards, mesh=mesh, in_specs=in_specs, out_specs=out_specs, check_vma=False)
```

```python
import jax
import jax.numpy as jnp
from jax import lax
from jax.experimental import pallas as pl
from jax.experimental.pallas import tpu as pltpu
from jax.sharding import PartitionSpec as P

SITE_DEV = 512
TAXO = 128
G = 64
NB = 40
LANES = 128
ROWS = 8
PART = 16
EVENT_BLOCK = 32
CODES = 1 << 17
SLANT = 13
HOLE = 1 << 24
COMPACT_ROWS = 16

COEFFS = ((1.0, 1.1, 1.0, 6.0, 0.004, 0.6), (0.3, 1.4, 0.9, 8.0, 0.002, 0.7))
LOW_LEVEL = -6.0
LEVEL_STEP = 0.1

AXES = ("ev", "site")
F32 = jnp.float32
BF16 = jnp.bfloat16
NT = (((1,), (1,)), ((), ()))

VMEM = pl.BlockSpec(memory_space=pltpu.VMEM)
SMEM = pl.BlockSpec(memory_space=pltpu.SMEM)
HBM = pl.BlockSpec(memory_space=pltpu.HBM)


def params(mebibytes):
    return pltpu.CompilerParams(vmem_limit_bytes=mebibytes << 20)


def parts_of(value):
    high = value.astype(BF16).astype(F32)
    rest = value - high
    middle = rest.astype(BF16).astype(F32)
    return high, middle, (rest - middle).astype(BF16).astype(F32)


def place_kernel(out_ref):
    out_ref[...] = lax.broadcasted_iota(jnp.int32, out_ref.shape, 1) - lax.broadcasted_iota(
        jnp.int32, out_ref.shape, 0
    )


def pack_kernel(n_ev, n_site, place_ref, rup_ref, idx_ref, eps_ref, out_ref):
    n_rup = rup_ref.shape[1]
    place = place_ref[0:6, :]
    spots = jnp.zeros((6, LANES), F32)
    for k in range(n_rup):
        spots = jnp.where(place == 6 * k, jnp.broadcast_to(rup_ref[:, k : k + 1], (6, LANES)), spots)
    row = jnp.broadcast_to(jnp.sum(spots, axis=0, keepdims=True), (2, LANES))
    lane = jnp.broadcast_to(place_ref[0:1, :], (2, LANES))
    row = jnp.where(lane == 6 * n_rup, idx_ref[0].astype(F32), row)
    high, middle, low = parts_of(row)
    row = (high + pltpu.roll(middle, PART, 1) + pltpu.roll(low, 2 * PART, 1)).astype(BF16)
    eps = eps_ref[...]

    def fill(i, carry):
        for j in range(n_site):
            out_ref[i * n_site + j, :, :SITE_DEV] = eps[:, j * SITE_DEV : (j + 1) * SITE_DEV]
            out_ref[i * n_site + j, :, SITE_DEV:] = row
        return carry

    lax.fori_loop(0, n_ev, fill, 0, unroll=n_ev <= 4)


def compact(own, code, value):
    rows = own.shape[0]
    above = lax.broadcasted_iota(jnp.int32, (rows, rows), 1) < lax.broadcasted_iota(jnp.int32, (rows, rows), 0)
    gaps = jnp.dot(above.astype(BF16), 1.0 - own.astype(BF16), preferred_element_type=F32).astype(jnp.int32)
    word = jnp.where(own, gaps * CODES + code, HOLE)
    size = 1
    while size < rows:
        bit = size * CODES
        from_word = jnp.concatenate([word[size:], jnp.full((size, LANES), HOLE, jnp.int32)], axis=0)
        from_value = jnp.concatenate([value[size:], jnp.zeros((size, LANES), F32)], axis=0)
        comes = (from_word & bit) != 0
        value = jnp.where(comes, from_value, value)
        word = jnp.where(comes, from_word, jnp.where((word & bit) != 0, HOLE, word))
        size *= 2
    return word, value


def slanted(array):
    return jnp.concatenate(
        [
            pltpu.roll(array[q : q + ROWS], (11 * q // ROWS) % 36, 1, stride=SLANT, stride_axis=0)
            for q in range(0, array.shape[0], ROWS)
        ],
        axis=0,
    )


def exposure_kernel(
    t_dev, rows, site_ref, taxo_ref, tract_ref, value_ref, vul_hbm, measure_hbm, offset_hbm,
    exp_ref, curve_ref, site_s, col_s, high_s, low_s, sum_s, curve_s, vul_ref, measure_ref, offset_ref, sems,
):
    copies = [
        pltpu.make_async_copy(source, target, sems.at[k])
        for k, (source, target) in enumerate(
            ((vul_hbm, vul_ref), (measure_hbm, measure_ref), (offset_hbm, offset_ref))
        )
    ]
    for copy in copies:
        copy.start()
    me = lax.axis_index("ev")
    first = me * t_dev
    n_col = exp_ref.shape[1]
    taxo = taxo_ref[...] - first
    own = (taxo >= 0) & (taxo < t_dev)
    code = site_ref[...] * n_col + tract_ref[...] * t_dev + taxo
    word, value = compact(own, code, value_ref[...])
    word, value = slanted(word), slanted(value)
    own = word != HOLE
    most = jnp.max(jnp.sum(own.astype(F32), axis=0, keepdims=True)).astype(jnp.int32)
    word, value = compact(own, word & (CODES - 1), value)
    high = value.astype(BF16).astype(F32)
    site_s[...] = ((word & (CODES - 1)) // n_col).astype(F32)
    col_s[...] = jnp.where((word & HOLE) != 0, -1, word & (n_col - 1)).astype(F32)
    high_s[...] = high
    low_s[...] = value - high

    level = lax.broadcasted_iota(jnp.int32, (256, LANES), 0).astype(F32).astype(BF16)
    zero = jnp.zeros((256, LANES), BF16)
    one = jnp.ones((256, LANES), BF16)

    def spread(ref, q, less=0.0):
        return jnp.broadcast_to((ref[pl.ds(q, 1), :] - less).astype(BF16), (256, LANES))

    def beside(parts):
        return jnp.concatenate(parts, axis=1)

    sum_s[...] = jnp.zeros_like(sum_s)

    def step(c, carry):
        site_rows = [[] for _ in range(SITE_DEV // 256)]
        high_rows, low_rows = [], []
        for u in range(rows):
            q = c * rows + u
            for part, found in enumerate(site_rows):
                found.append(jnp.where(level == spread(site_s, q, 256.0 * part), one, zero))
            here = level == spread(col_s, q)
            high_rows.append(jnp.where(here, spread(high_s, q), zero))
            low_rows.append(jnp.where(here, spread(low_s, q), zero))
        at_site = jnp.concatenate([beside(found) for found in site_rows], axis=0)
        sum_s[...] += lax.dot_general(
            beside([at_site, at_site]), beside(high_rows + low_rows), NT, preferred_element_type=F32
        )
        return carry

    lax.fori_loop(0, (most + rows - 1) // rows, step, 0)
    exp_ref[...] = sum_s[...].astype(BF16)

    for copy in copies:
        copy.wait()
    vul = vul_ref[...].astype(F32)
    table = jnp.concatenate([vul, jnp.broadcast_to(vul[NB - 1 : NB], (G - NB, TAXO))], axis=0)
    offset = jnp.broadcast_to(offset_ref[...], (G, TAXO))
    level_row = lax.broadcasted_iota(jnp.int32, (G, TAXO), 0)
    for bit in range(5):
        size = 1 << bit
        moved = jnp.where(level_row >= size, pltpu.roll(table, size, 0), 0.0)
        table = jnp.where((offset & size) != 0, moved, table)
    measure = jnp.broadcast_to(measure_ref[...], (G, TAXO))
    both = jnp.concatenate(
        [jnp.where(measure == 0, table, 0.0), jnp.where(measure == 1, table, 0.0)], axis=0
    )
    curve_s[...] = both.T
    curve_ref[...] = curve_s[pl.ds(pl.multiple_of(first, ROWS), t_dev), :].astype(BF16)


def swap_groups(block, groups, width):
    total = block.shape[0]
    high = total // groups
    row_group = lax.broadcasted_iota(jnp.int32, block.shape, 0) // high
    lane_group = lax.broadcasted_iota(jnp.int32, block.shape, 1) // width
    result = block
    for d in range(1, groups):
        moved = pltpu.roll(pltpu.roll(block, total - high * d, 0), width * d, 1)
        gap = lane_group - row_group
        result = jnp.where((gap == d) | (gap == d - groups), moved, result)
    return result


def loss_kernel(n_ev, n_site, n_rup, got_ref, coords_ref, exp_ref, curve_ref, out_ref, geo_s, ratio_s, loss_s):
    n_dev = n_ev * n_site
    t_dev = curve_ref.shape[0]
    n_col = exp_ref.shape[1]
    events = n_dev
    ev_dev = events // n_ev
    me = lax.axis_index("site")
    start = pl.multiple_of(me * SITE_DEV, LANES)
    x = coords_ref[0:1, pl.ds(start, SITE_DEV)]
    y = coords_ref[1:2, pl.ds(start, SITE_DEV)]

    every = got_ref[:, :, SITE_DEV:].astype(F32)[:, 0, :]
    geo_s[...] = every
    table = jnp.concatenate(
        [
            every if u == 0 and p == 0 else pltpu.roll(every, LANES - 6 * u - PART * p, 1)
            for p in range(3)
            for u in range(n_rup)
        ],
        axis=0,
    ).astype(BF16)
    level = lax.broadcasted_iota(jnp.int32, (G, SITE_DEV), 0).astype(F32).astype(BF16)
    level_less = (lax.broadcasted_iota(jnp.int32, (G, SITE_DEV), 0) - 1).astype(F32).astype(BF16)
    zero = jnp.zeros((G, SITE_DEV), BF16)
    curve = curve_ref[...]
    exposure = exp_ref[...]
    diagonal = lax.broadcasted_iota(jnp.int32, (t_dev, n_col), 0) == (
        lax.broadcasted_iota(jnp.int32, (t_dev, n_col), 1) % t_dev
    )

    def joined(array):
        return (array + pltpu.roll(array, LANES - PART, 1)) + pltpu.roll(array, LANES - 2 * PART, 1)

    def block(b, carry):
        first = pl.multiple_of(b * EVENT_BLOCK, EVENT_BLOCK)
        here = joined(geo_s[pl.ds(first, EVENT_BLOCK), :])
        rupture = here[:, 6 * n_rup : 6 * n_rup + 1].astype(jnp.int32)
        place = lax.broadcasted_iota(jnp.int32, (EVENT_BLOCK, n_dev), 1) * n_rup
        hot = jnp.concatenate([(place + u == rupture).astype(BF16) for u in range(n_rup)] * 3, axis=1)
        own = jnp.dot(hot, table, preferred_element_type=F32)
        start_x = own[:, 0:1]
        start_y = own[:, 1:2]
        along_x = own[:, 2:3] - start_x
        along_y = own[:, 3:4] - start_y
        depth = own[:, 4:5]
        size = own[:, 5:6]
        length_sq = along_x * along_x + along_y * along_y
        rel_x = x - start_x
        rel_y = y - start_y
        portion = jnp.clip((rel_x * along_x + rel_y * along_y) / length_sq, 0.0, 1.0)
        off_x = rel_x - portion * along_x
        off_y = rel_y - portion * along_y
        distance = jnp.sqrt(off_x * off_x + off_y * off_y + depth * depth)
        got = got_ref[pl.ds(b * EVENT_BLOCK, EVENT_BLOCK), :, :SITE_DEV].astype(F32)
        below, weight_0, weight_1 = [], [], []
        for k in range(2):
            c = COEFFS[k]
            eps = got[:, k, :]
            field = (
                c[0] + c[1] * (size - 6.0)
                - c[2] * 0.5 * jnp.log(distance * distance + c[3] * c[3])
                - c[4] * distance
                + c[5] * eps
            )
            position = jnp.clip((field - LOW_LEVEL) / LEVEL_STEP, 0.0, G - 1.0)
            floor = jnp.floor(position)
            below.append(floor)
            weight_0.append(1.0 - (position - floor))
            weight_1.append(jnp.maximum(0.0, 1.0 - ((floor + 1.0) - position)))

        def wide(array, e):
            return jnp.broadcast_to(array[e : e + 1].astype(BF16), (G, SITE_DEV))

        ratios = []
        for e in range(EVENT_BLOCK):
            tents = []
            for k in range(2):
                at = wide(below[k], e)
                tents.append(
                    jnp.where(
                        level == at,
                        wide(weight_0[k], e),
                        jnp.where(level_less == at, wide(weight_1[k], e), zero),
                    )
                )
            ratio = jnp.dot(curve, jnp.concatenate(tents, axis=0), preferred_element_type=F32)
            ratios.append(ratio.astype(BF16))
            if len(ratios) * t_dev == 32:
                ratio_s[(e + 1) * t_dev - 32 : (e + 1) * t_dev, :] = jnp.concatenate(ratios, axis=0)
                ratios = []
        terms = jnp.dot(ratio_s[...], exposure, preferred_element_type=F32)
        rows = [
            jnp.sum(jnp.where(diagonal, terms[e * t_dev : (e + 1) * t_dev], 0.0), axis=0, keepdims=True)
            for e in range(EVENT_BLOCK)
        ]
        loss_s[pl.ds(first, EVENT_BLOCK), :] = jnp.concatenate(rows, axis=0)
        return carry

    lax.fori_loop(0, events // EVENT_BLOCK, block, 0)

    halves = n_col // LANES

    def arrange(i, carry):
        first = pl.multiple_of(i * ev_dev, ROWS)
        for u in range(halves):
            part = loss_s[pl.ds(first, ev_dev), u * LANES : (u + 1) * LANES]
            out_ref[pl.ds(pl.multiple_of((i * halves + u) * ev_dev, ROWS), ev_dev), :] = swap_groups(
                part, n_ev, t_dev
            )
        return carry

    lax.fori_loop(0, n_ev, arrange, 0, unroll=n_ev <= 4)


def total_kernel(n_ev, n_site, got_ref, out_ref):
    high = got_ref.shape[0] // (n_ev * n_site)
    rows = []
    for i in range(n_ev):
        for h in range(high):
            part = got_ref[pl.ds(i * n_site * high + h, n_site, stride=high), :]
            rows.append(jnp.sum(part, axis=0, keepdims=True))
    out_ref[...] = swap_groups(jnp.concatenate(rows, axis=0), n_ev, LANES // n_ev)


def shards(
    ruptures,
    event_rupture,
    epsilon,
    site_coords,
    vulnerability,
    taxo_measure,
    taxo_offset,
    asset_site,
    asset_taxo,
    asset_tract,
    asset_value,
):
    n_ev = lax.axis_size("ev")
    n_site = lax.axis_size("site")
    n_dev = n_ev * n_site
    n_rup = ruptures.shape[1]
    sites = epsilon.shape[2]
    t_dev = TAXO // n_ev
    n_col = n_site * t_dev
    asset_rows = asset_site.shape[0] // LANES

    def stays(array):
        return pltpu.with_memory_space_constraint(array, pltpu.HBM)

    def exchange(array):
        return lax.all_to_all(array, AXES, split_axis=0, concat_axis=0, tiled=True)

    place = pl.pallas_call(
        place_kernel,
        out_shape=jax.ShapeDtypeStruct((ROWS, LANES), jnp.int32),
        out_specs=VMEM,
        compiler_params=params(4),
        cost_estimate=pl.CostEstimate(flops=4_000_000_000, bytes_accessed=12_000_000, transcendentals=0),
    )()
    packed = pl.pallas_call(
        lambda *refs: pack_kernel(n_ev, n_site, *refs),
        out_shape=jax.ShapeDtypeStruct((n_dev, 2, SITE_DEV + LANES), BF16),
        in_specs=[VMEM, VMEM, SMEM, VMEM],
        out_specs=VMEM,
        compiler_params=params(4),
    )(place, ruptures, event_rupture, epsilon.reshape(2, sites))
    got = exchange(packed)

    def as_rows(array):
        return array.reshape(asset_rows, LANES)

    exposure, curve = pl.pallas_call(
        lambda *refs: exposure_kernel(t_dev, COMPACT_ROWS, *refs),
        out_shape=(
            jax.ShapeDtypeStruct((SITE_DEV, n_col), BF16),
            jax.ShapeDtypeStruct((t_dev, 2 * G), BF16),
        ),
        in_specs=[VMEM] * 4 + [HBM] * 3,
        out_specs=(VMEM, VMEM),
        scratch_shapes=[pltpu.VMEM((asset_rows, LANES), F32)] * 4
        + [pltpu.VMEM((SITE_DEV, n_col), F32), pltpu.VMEM((TAXO, 2 * G), F32)]
        + [pltpu.VMEM((NB, TAXO), BF16), pltpu.VMEM((1, TAXO), jnp.int32), pltpu.VMEM((1, TAXO), jnp.int32)]
        + [pltpu.SemaphoreType.DMA((3,))],
        compiler_params=params(24),
        cost_estimate=pl.CostEstimate(
            flops=2 * asset_rows * LANES * SITE_DEV * n_col, bytes_accessed=1 << 20, transcendentals=0
        ),
    )(
        as_rows(asset_site),
        as_rows(asset_taxo),
        as_rows(asset_tract),
        as_rows(asset_value),
        stays(vulnerability.T),
        stays(taxo_measure.reshape(1, TAXO)),
        stays(taxo_offset.reshape(1, TAXO)),
    )

    parts = pl.pallas_call(
        lambda *refs: loss_kernel(n_ev, n_site, n_rup, *refs),
        out_shape=jax.ShapeDtypeStruct((n_dev * n_col // LANES, LANES), F32),
        in_specs=[VMEM] * 4,
        out_specs=VMEM,
        scratch_shapes=[
            pltpu.VMEM((n_dev, LANES), F32),
            pltpu.VMEM((EVENT_BLOCK * t_dev, SITE_DEV), BF16),
            pltpu.VMEM((n_dev, n_col), F32),
        ],
        compiler_params=params(20),
    )(got, site_coords, exposure, curve)

    losses = pl.pallas_call(
        lambda *refs: total_kernel(n_ev, n_site, *refs),
        out_shape=jax.ShapeDtypeStruct((n_dev // n_ev, LANES), F32),
        in_specs=[VMEM],
        out_specs=VMEM,
        compiler_params=params(4),
    )(exchange(parts))
    return losses[None]


def solution(mesh):
    in_specs = (
        P(None, ("ev", "site")),
        P(("ev", "site")),
        P(None, ("ev", "site"), None),
        P(),
        P(),
        P(),
        P(),
        P("site"),
        P("site"),
        P("site"),
        P("site"),
    )
    out_specs = P("site", "ev", None)
    return jax.shard_map(shards, mesh=mesh, in_specs=in_specs, out_specs=out_specs, check_vma=False)
```

```python
import jax
import jax.numpy as jnp
from jax import lax
from jax.experimental import pallas as pl
from jax.experimental.pallas import tpu as pltpu
from jax.sharding import PartitionSpec as P

SITE_DEV = 512
TAXO = 128
G = 64
NB = 40
LANES = 128
ROWS = 8
PART = 16
EVENT_BLOCK = 32
CODES = 1 << 17
SLANT = 13
HOLE = 1 << 24
COMPACT_ROWS = 10

COEFFS = ((1.0, 1.1, 1.0, 6.0, 0.004, 0.6), (0.3, 1.4, 0.9, 8.0, 0.002, 0.7))
LOW_LEVEL = -6.0
LEVEL_STEP = 0.1

AXES = ("ev", "site")
F32 = jnp.float32
BF16 = jnp.bfloat16
NT = (((1,), (1,)), ((), ()))

VMEM = pl.BlockSpec(memory_space=pltpu.VMEM)
SMEM = pl.BlockSpec(memory_space=pltpu.SMEM)
HBM = pl.BlockSpec(memory_space=pltpu.HBM)


def params(mebibytes):
    return pltpu.CompilerParams(vmem_limit_bytes=mebibytes << 20)


def parts_of(value):
    high = value.astype(BF16).astype(F32)
    rest = value - high
    middle = rest.astype(BF16).astype(F32)
    return high, middle, (rest - middle).astype(BF16).astype(F32)


def place_kernel(out_ref):
    out_ref[...] = lax.broadcasted_iota(jnp.int32, out_ref.shape, 1) - lax.broadcasted_iota(
        jnp.int32, out_ref.shape, 0
    )


def pack_kernel(n_ev, n_site, place_ref, rup_ref, idx_ref, eps_ref, out_ref):
    n_rup = rup_ref.shape[1]
    place = place_ref[0:6, :]
    spots = jnp.zeros((6, LANES), F32)
    for k in range(n_rup):
        spots = jnp.where(place == 6 * k, jnp.broadcast_to(rup_ref[:, k : k + 1], (6, LANES)), spots)
    row = jnp.broadcast_to(jnp.sum(spots, axis=0, keepdims=True), (2, LANES))
    lane = jnp.broadcast_to(place_ref[0:1, :], (2, LANES))
    row = jnp.where(lane == 6 * n_rup, idx_ref[0].astype(F32), row)
    high, middle, low = parts_of(row)
    row = (high + pltpu.roll(middle, PART, 1) + pltpu.roll(low, 2 * PART, 1)).astype(BF16)
    eps = eps_ref[...]

    def fill(i, carry):
        for j in range(n_site):
            out_ref[i * n_site + j, :, :SITE_DEV] = eps[:, j * SITE_DEV : (j + 1) * SITE_DEV]
            out_ref[i * n_site + j, :, SITE_DEV:] = row
        return carry

    lax.fori_loop(0, n_ev, fill, 0, unroll=n_ev <= 4)


def compact(own, code, value):
    rows = own.shape[0]
    above = lax.broadcasted_iota(jnp.int32, (rows, rows), 1) < lax.broadcasted_iota(jnp.int32, (rows, rows), 0)
    gaps = jnp.dot(above.astype(BF16), 1.0 - own.astype(BF16), preferred_element_type=F32).astype(jnp.int32)
    word = jnp.where(own, gaps * CODES + code, HOLE)
    size = 1
    while size < rows:
        bit = size * CODES
        from_word = jnp.concatenate([word[size:], jnp.full((size, LANES), HOLE, jnp.int32)], axis=0)
        from_value = jnp.concatenate([value[size:], jnp.zeros((size, LANES), F32)], axis=0)
        comes = (from_word & bit) != 0
        value = jnp.where(comes, from_value, value)
        word = jnp.where(comes, from_word, jnp.where((word & bit) != 0, HOLE, word))
        size *= 2
    return word, value


def slanted(array):
    return jnp.concatenate(
        [
            pltpu.roll(array[q : q + ROWS], (11 * q // ROWS) % 36, 1, stride=SLANT, stride_axis=0)
            for q in range(0, array.shape[0], ROWS)
        ],
        axis=0,
    )


def exposure_kernel(
    t_dev, rows, site_ref, taxo_ref, tract_ref, value_ref, vul_hbm, measure_hbm, offset_hbm,
    exp_ref, curve_ref, site_s, col_s, high_s, low_s, sum_s, curve_s, vul_ref, measure_ref, offset_ref, sems,
):
    copies = [
        pltpu.make_async_copy(source, target, sems.at[k])
        for k, (source, target) in enumerate(
            ((vul_hbm, vul_ref), (measure_hbm, measure_ref), (offset_hbm, offset_ref))
        )
    ]
    for copy in copies:
        copy.start()
    me = lax.axis_index("ev")
    first = me * t_dev
    n_col = exp_ref.shape[1]
    taxo = taxo_ref[...] - first
    own = (taxo >= 0) & (taxo < t_dev)
    code = site_ref[...] * n_col + tract_ref[...] * t_dev + taxo
    word, value = compact(own, code, value_ref[...])
    word, value = slanted(word), slanted(value)
    own = word != HOLE
    most = jnp.max(jnp.sum(own.astype(F32), axis=0, keepdims=True)).astype(jnp.int32)
    word, value = compact(own, word & (CODES - 1), value)
    high = value.astype(BF16).astype(F32)
    site_s[...] = ((word & (CODES - 1)) // n_col).astype(F32)
    col_s[...] = jnp.where((word & HOLE) != 0, -1, word & (n_col - 1)).astype(F32)
    high_s[...] = high
    low_s[...] = value - high

    level = lax.broadcasted_iota(jnp.int32, (256, LANES), 0).astype(F32).astype(BF16)
    zero = jnp.zeros((256, LANES), BF16)
    one = jnp.ones((256, LANES), BF16)

    def spread(ref, q, less=0.0):
        return jnp.broadcast_to((ref[pl.ds(q, 1), :] - less).astype(BF16), (256, LANES))

    def beside(parts):
        return jnp.concatenate(parts, axis=1)

    sum_s[...] = jnp.zeros_like(sum_s)

    def step(c, carry):
        site_rows = [[] for _ in range(SITE_DEV // 256)]
        high_rows, low_rows = [], []
        for u in range(rows):
            q = c * rows + u
            for part, found in enumerate(site_rows):
                found.append(jnp.where(level == spread(site_s, q, 256.0 * part), one, zero))
            here = level == spread(col_s, q)
            high_rows.append(jnp.where(here, spread(high_s, q), zero))
            low_rows.append(jnp.where(here, spread(low_s, q), zero))
        at_site = jnp.concatenate([beside(found) for found in site_rows], axis=0)
        sum_s[...] += lax.dot_general(
            beside([at_site, at_site]), beside(high_rows + low_rows), NT, preferred_element_type=F32
        )
        return carry

    lax.fori_loop(0, (most + rows - 1) // rows, step, 0)
    exp_ref[...] = sum_s[...].astype(BF16)

    for copy in copies:
        copy.wait()
    vul = vul_ref[...].astype(F32)
    table = jnp.concatenate([vul, jnp.broadcast_to(vul[NB - 1 : NB], (G - NB, TAXO))], axis=0)
    offset = jnp.broadcast_to(offset_ref[...], (G, TAXO))
    level_row = lax.broadcasted_iota(jnp.int32, (G, TAXO), 0)
    for bit in range(5):
        size = 1 << bit
        moved = jnp.where(level_row >= size, pltpu.roll(table, size, 0), 0.0)
        table = jnp.where((offset & size) != 0, moved, table)
    measure = jnp.broadcast_to(measure_ref[...], (G, TAXO))
    both = jnp.concatenate(
        [jnp.where(measure == 0, table, 0.0), jnp.where(measure == 1, table, 0.0)], axis=0
    )
    curve_s[...] = both.T
    curve_ref[...] = curve_s[pl.ds(pl.multiple_of(first, ROWS), t_dev), :].astype(BF16)


def swap_groups(block, groups, width):
    total = block.shape[0]
    high = total // groups
    row_group = lax.broadcasted_iota(jnp.int32, block.shape, 0) // high
    lane_group = lax.broadcasted_iota(jnp.int32, block.shape, 1) // width
    result = block
    for d in range(1, groups):
        moved = pltpu.roll(pltpu.roll(block, total - high * d, 0), width * d, 1)
        gap = lane_group - row_group
        result = jnp.where((gap == d) | (gap == d - groups), moved, result)
    return result


def loss_kernel(n_ev, n_site, n_rup, got_ref, coords_ref, exp_ref, curve_ref, out_ref, geo_s, ratio_s, loss_s):
    n_dev = n_ev * n_site
    t_dev = curve_ref.shape[0]
    n_col = exp_ref.shape[1]
    events = n_dev
    ev_dev = events // n_ev
    me = lax.axis_index("site")
    start = pl.multiple_of(me * SITE_DEV, LANES)
    x = coords_ref[0:1, pl.ds(start, SITE_DEV)]
    y = coords_ref[1:2, pl.ds(start, SITE_DEV)]

    every = got_ref[:, :, SITE_DEV:].astype(F32)[:, 0, :]
    geo_s[...] = every
    table = jnp.concatenate(
        [
            every if u == 0 and p == 0 else pltpu.roll(every, LANES - 6 * u - PART * p, 1)
            for p in range(3)
            for u in range(n_rup)
        ],
        axis=0,
    ).astype(BF16)
    level = lax.broadcasted_iota(jnp.int32, (G, SITE_DEV), 0).astype(F32).astype(BF16)
    level_less = (lax.broadcasted_iota(jnp.int32, (G, SITE_DEV), 0) - 1).astype(F32).astype(BF16)
    zero = jnp.zeros((G, SITE_DEV), BF16)
    curve = curve_ref[...]
    exposure = exp_ref[...]
    diagonal = lax.broadcasted_iota(jnp.int32, (t_dev, n_col), 0) == (
        lax.broadcasted_iota(jnp.int32, (t_dev, n_col), 1) % t_dev
    )

    def joined(array):
        return (array + pltpu.roll(array, LANES - PART, 1)) + pltpu.roll(array, LANES - 2 * PART, 1)

    def block(b, carry):
        first = pl.multiple_of(b * EVENT_BLOCK, EVENT_BLOCK)
        here = joined(geo_s[pl.ds(first, EVENT_BLOCK), :])
        rupture = here[:, 6 * n_rup : 6 * n_rup + 1].astype(jnp.int32)
        place = lax.broadcasted_iota(jnp.int32, (EVENT_BLOCK, n_dev), 1) * n_rup
        hot = jnp.concatenate([(place + u == rupture).astype(BF16) for u in range(n_rup)] * 3, axis=1)
        own = jnp.dot(hot, table, preferred_element_type=F32)
        start_x = own[:, 0:1]
        start_y = own[:, 1:2]
        along_x = own[:, 2:3] - start_x
        along_y = own[:, 3:4] - start_y
        depth = own[:, 4:5]
        size = own[:, 5:6]
        length_sq = along_x * along_x + along_y * along_y
        rel_x = x - start_x
        rel_y = y - start_y
        portion = jnp.clip((rel_x * along_x + rel_y * along_y) / length_sq, 0.0, 1.0)
        off_x = rel_x - portion * along_x
        off_y = rel_y - portion * along_y
        distance = jnp.sqrt(off_x * off_x + off_y * off_y + depth * depth)
        got = got_ref[pl.ds(b * EVENT_BLOCK, EVENT_BLOCK), :, :SITE_DEV].astype(F32)
        below, weight_0, weight_1 = [], [], []
        for k in range(2):
            c = COEFFS[k]
            eps = got[:, k, :]
            field = (
                c[0] + c[1] * (size - 6.0)
                - c[2] * 0.5 * jnp.log(distance * distance + c[3] * c[3])
                - c[4] * distance
                + c[5] * eps
            )
            position = jnp.clip((field - LOW_LEVEL) / LEVEL_STEP, 0.0, G - 1.0)
            floor = jnp.floor(position)
            below.append(floor)
            weight_0.append(1.0 - (position - floor))
            weight_1.append(jnp.maximum(0.0, 1.0 - ((floor + 1.0) - position)))

        def wide(array, e):
            return jnp.broadcast_to(array[e : e + 1].astype(BF16), (G, SITE_DEV))

        ratios = []
        for e in range(EVENT_BLOCK):
            tents = []
            for k in range(2):
                at = wide(below[k], e)
                tents.append(
                    jnp.where(
                        level == at,
                        wide(weight_0[k], e),
                        jnp.where(level_less == at, wide(weight_1[k], e), zero),
                    )
                )
            ratio = jnp.dot(curve, jnp.concatenate(tents, axis=0), preferred_element_type=F32)
            ratios.append(ratio.astype(BF16))
            if len(ratios) * t_dev == 32:
                ratio_s[(e + 1) * t_dev - 32 : (e + 1) * t_dev, :] = jnp.concatenate(ratios, axis=0)
                ratios = []
        terms = jnp.dot(ratio_s[...], exposure, preferred_element_type=F32)
        rows = [
            jnp.sum(jnp.where(diagonal, terms[e * t_dev : (e + 1) * t_dev], 0.0), axis=0, keepdims=True)
            for e in range(EVENT_BLOCK)
        ]
        loss_s[pl.ds(first, EVENT_BLOCK), :] = jnp.concatenate(rows, axis=0)
        return carry

    lax.fori_loop(0, events // EVENT_BLOCK, block, 0)

    halves = n_col // LANES

    def arrange(i, carry):
        first = pl.multiple_of(i * ev_dev, ROWS)
        for u in range(halves):
            part = loss_s[pl.ds(first, ev_dev), u * LANES : (u + 1) * LANES]
            out_ref[pl.ds(pl.multiple_of((i * halves + u) * ev_dev, ROWS), ev_dev), :] = swap_groups(
                part, n_ev, t_dev
            )
        return carry

    lax.fori_loop(0, n_ev, arrange, 0, unroll=n_ev <= 4)


def total_kernel(n_ev, n_site, got_ref, out_ref):
    high = got_ref.shape[0] // (n_ev * n_site)
    rows = []
    for i in range(n_ev):
        for h in range(high):
            part = got_ref[pl.ds(i * n_site * high + h, n_site, stride=high), :]
            rows.append(jnp.sum(part, axis=0, keepdims=True))
    out_ref[...] = swap_groups(jnp.concatenate(rows, axis=0), n_ev, LANES // n_ev)


def shards(
    ruptures,
    event_rupture,
    epsilon,
    site_coords,
    vulnerability,
    taxo_measure,
    taxo_offset,
    asset_site,
    asset_taxo,
    asset_tract,
    asset_value,
):
    n_ev = lax.axis_size("ev")
    n_site = lax.axis_size("site")
    n_dev = n_ev * n_site
    n_rup = ruptures.shape[1]
    sites = epsilon.shape[2]
    t_dev = TAXO // n_ev
    n_col = n_site * t_dev
    asset_rows = asset_site.shape[0] // LANES

    def stays(array):
        return pltpu.with_memory_space_constraint(array, pltpu.HBM)

    def exchange(array):
        return lax.all_to_all(array, AXES, split_axis=0, concat_axis=0, tiled=True)

    place = pl.pallas_call(
        place_kernel,
        out_shape=jax.ShapeDtypeStruct((ROWS, LANES), jnp.int32),
        out_specs=VMEM,
        compiler_params=params(4),
        cost_estimate=pl.CostEstimate(flops=4_000_000_000, bytes_accessed=12_000_000, transcendentals=0),
    )()
    packed = pl.pallas_call(
        lambda *refs: pack_kernel(n_ev, n_site, *refs),
        out_shape=jax.ShapeDtypeStruct((n_dev, 2, SITE_DEV + LANES), BF16),
        in_specs=[VMEM, VMEM, SMEM, VMEM],
        out_specs=VMEM,
        compiler_params=params(4),
    )(place, ruptures, event_rupture, epsilon.reshape(2, sites))
    got = exchange(packed)

    def as_rows(array):
        return array.reshape(asset_rows, LANES)

    exposure, curve = pl.pallas_call(
        lambda *refs: exposure_kernel(t_dev, COMPACT_ROWS, *refs),
        out_shape=(
            jax.ShapeDtypeStruct((SITE_DEV, n_col), BF16),
            jax.ShapeDtypeStruct((t_dev, 2 * G), BF16),
        ),
        in_specs=[VMEM] * 4 + [HBM] * 3,
        out_specs=(VMEM, VMEM),
        scratch_shapes=[pltpu.VMEM((asset_rows, LANES), F32)] * 4
        + [pltpu.VMEM((SITE_DEV, n_col), F32), pltpu.VMEM((TAXO, 2 * G), F32)]
        + [pltpu.VMEM((NB, TAXO), BF16), pltpu.VMEM((1, TAXO), jnp.int32), pltpu.VMEM((1, TAXO), jnp.int32)]
        + [pltpu.SemaphoreType.DMA((3,))],
        compiler_params=params(24),
        cost_estimate=pl.CostEstimate(
            flops=2 * asset_rows * LANES * SITE_DEV * n_col, bytes_accessed=1 << 20, transcendentals=0
        ),
    )(
        as_rows(asset_site),
        as_rows(asset_taxo),
        as_rows(asset_tract),
        as_rows(asset_value),
        stays(vulnerability.T),
        stays(taxo_measure.reshape(1, TAXO)),
        stays(taxo_offset.reshape(1, TAXO)),
    )

    parts = pl.pallas_call(
        lambda *refs: loss_kernel(n_ev, n_site, n_rup, *refs),
        out_shape=jax.ShapeDtypeStruct((n_dev * n_col // LANES, LANES), F32),
        in_specs=[VMEM] * 4,
        out_specs=VMEM,
        scratch_shapes=[
            pltpu.VMEM((n_dev, LANES), F32),
            pltpu.VMEM((EVENT_BLOCK * t_dev, SITE_DEV), BF16),
            pltpu.VMEM((n_dev, n_col), F32),
        ],
        compiler_params=params(20),
    )(got, site_coords, exposure, curve)

    losses = pl.pallas_call(
        lambda *refs: total_kernel(n_ev, n_site, *refs),
        out_shape=jax.ShapeDtypeStruct((n_dev // n_ev, LANES), F32),
        in_specs=[VMEM],
        out_specs=VMEM,
        compiler_params=params(4),
    )(exchange(parts))
    return losses[None]


def solution(mesh):
    in_specs = (
        P(None, ("ev", "site")),
        P(("ev", "site")),
        P(None, ("ev", "site"), None),
        P(),
        P(),
        P(),
        P(),
        P("site"),
        P("site"),
        P("site"),
        P("site"),
    )
    out_specs = P("site", "ev", None)
    return jax.shard_map(shards, mesh=mesh, in_specs=in_specs, out_specs=out_specs, check_vma=False)
```

```python
import jax
import jax.numpy as jnp
from jax import lax
from jax.experimental import pallas as pl
from jax.experimental.pallas import tpu as pltpu
from jax.sharding import PartitionSpec as P

SITE_DEV = 512
TAXO = 128
G = 64
NB = 40
LANES = 128
ROWS = 8
PART = 16
EVENT_BLOCK = 32
CODES = 1 << 17
SLANT = 13
HOLE = 1 << 24
COMPACT_ROWS = 10

COEFFS = ((1.0, 1.1, 1.0, 6.0, 0.004, 0.6), (0.3, 1.4, 0.9, 8.0, 0.002, 0.7))
LOW_LEVEL = -6.0
LEVEL_STEP = 0.1

AXES = ("ev", "site")
F32 = jnp.float32
BF16 = jnp.bfloat16
NT = (((1,), (1,)), ((), ()))

VMEM = pl.BlockSpec(memory_space=pltpu.VMEM)
SMEM = pl.BlockSpec(memory_space=pltpu.SMEM)
HBM = pl.BlockSpec(memory_space=pltpu.HBM)


def params(mebibytes):
    return pltpu.CompilerParams(vmem_limit_bytes=mebibytes << 20)


def parts_of(value):
    high = value.astype(BF16).astype(F32)
    rest = value - high
    middle = rest.astype(BF16).astype(F32)
    return high, middle, (rest - middle).astype(BF16).astype(F32)


def place_kernel(out_ref):
    out_ref[...] = lax.broadcasted_iota(jnp.int32, out_ref.shape, 1) - lax.broadcasted_iota(
        jnp.int32, out_ref.shape, 0
    )


def pack_kernel(n_ev, n_site, place_ref, rup_ref, idx_ref, eps_ref, out_ref):
    n_rup = rup_ref.shape[1]
    place = place_ref[0:6, :]
    spots = jnp.zeros((6, LANES), F32)
    for k in range(n_rup):
        spots = jnp.where(place == 6 * k, jnp.broadcast_to(rup_ref[:, k : k + 1], (6, LANES)), spots)
    row = jnp.broadcast_to(jnp.sum(spots, axis=0, keepdims=True), (2, LANES))
    lane = jnp.broadcast_to(place_ref[0:1, :], (2, LANES))
    row = jnp.where(lane == 6 * n_rup, idx_ref[0].astype(F32), row)
    high, middle, low = parts_of(row)
    row = (high + pltpu.roll(middle, PART, 1) + pltpu.roll(low, 2 * PART, 1)).astype(BF16)
    eps = eps_ref[...]

    def fill(i, carry):
        for j in range(n_site):
            own = eps[:, j * SITE_DEV : (j + 1) * SITE_DEV]
            out_ref[i * n_site + j] = jnp.concatenate([own, row], axis=1)
        return carry

    lax.fori_loop(0, n_ev, fill, 0, unroll=n_ev <= 4)


def compact(own, code, value):
    rows = own.shape[0]
    above = lax.broadcasted_iota(jnp.int32, (rows, rows), 1) < lax.broadcasted_iota(jnp.int32, (rows, rows), 0)
    gaps = jnp.dot(above.astype(BF16), 1.0 - own.astype(BF16), preferred_element_type=F32).astype(jnp.int32)
    word = jnp.where(own, gaps * CODES + code, HOLE)
    size = 1
    while size < rows:
        bit = size * CODES
        from_word = jnp.concatenate([word[size:], jnp.full((size, LANES), HOLE, jnp.int32)], axis=0)
        from_value = jnp.concatenate([value[size:], jnp.zeros((size, LANES), F32)], axis=0)
        comes = (from_word & bit) != 0
        value = jnp.where(comes, from_value, value)
        word = jnp.where(comes, from_word, jnp.where((word & bit) != 0, HOLE, word))
        size *= 2
    return word, value


def slanted(array):
    return jnp.concatenate(
        [
            pltpu.roll(array[q : q + ROWS], (11 * q // ROWS) % 36, 1, stride=SLANT, stride_axis=0)
            for q in range(0, array.shape[0], ROWS)
        ],
        axis=0,
    )


def exposure_kernel(
    t_dev, rows, site_ref, taxo_ref, tract_ref, value_ref, vul_hbm, measure_hbm, offset_hbm,
    exp_ref, curve_ref, site_s, col_s, high_s, low_s, sum_s, curve_s, vul_ref, measure_ref, offset_ref, sems,
):
    copies = [
        pltpu.make_async_copy(source, target, sems.at[k])
        for k, (source, target) in enumerate(
            ((vul_hbm, vul_ref), (measure_hbm, measure_ref), (offset_hbm, offset_ref))
        )
    ]
    for copy in copies:
        copy.start()
    me = lax.axis_index("ev")
    first = me * t_dev
    n_col = exp_ref.shape[1]
    taxo = taxo_ref[...] - first
    own = (taxo >= 0) & (taxo < t_dev)
    code = site_ref[...] * n_col + tract_ref[...] * t_dev + taxo
    word, value = compact(own, code, value_ref[...])
    word, value = slanted(word), slanted(value)
    own = word != HOLE
    most = jnp.max(jnp.sum(own.astype(F32), axis=0, keepdims=True)).astype(jnp.int32)
    word, value = compact(own, word & (CODES - 1), value)
    high = value.astype(BF16).astype(F32)
    site_s[...] = ((word & (CODES - 1)) // n_col).astype(F32)
    col_s[...] = jnp.where((word & HOLE) != 0, -1, word & (n_col - 1)).astype(F32)
    high_s[...] = high
    low_s[...] = value - high

    level = lax.broadcasted_iota(jnp.int32, (256, LANES), 0).astype(F32).astype(BF16)
    zero = jnp.zeros((256, LANES), BF16)
    one = jnp.ones((256, LANES), BF16)

    def spread(ref, q, less=0.0):
        return jnp.broadcast_to((ref[pl.ds(q, 1), :] - less).astype(BF16), (256, LANES))

    def beside(parts):
        return jnp.concatenate(parts, axis=1)

    sum_s[...] = jnp.zeros_like(sum_s)

    def step(c, carry):
        site_rows = [[] for _ in range(SITE_DEV // 256)]
        high_rows, low_rows = [], []
        for u in range(rows):
            q = c * rows + u
            for part, found in enumerate(site_rows):
                found.append(jnp.where(level == spread(site_s, q, 256.0 * part), one, zero))
            here = level == spread(col_s, q)
            high_rows.append(jnp.where(here, spread(high_s, q), zero))
            low_rows.append(jnp.where(here, spread(low_s, q), zero))
        at_site = jnp.concatenate([beside(found) for found in site_rows], axis=0)
        sum_s[...] += lax.dot_general(
            beside([at_site, at_site]), beside(high_rows + low_rows), NT, preferred_element_type=F32
        )
        return carry

    lax.fori_loop(0, (most + rows - 1) // rows, step, 0)
    exp_ref[...] = sum_s[...].astype(BF16)

    for copy in copies:
        copy.wait()
    vul = vul_ref[...].astype(F32)
    table = jnp.concatenate([vul, jnp.broadcast_to(vul[NB - 1 : NB], (G - NB, TAXO))], axis=0)
    offset = jnp.broadcast_to(offset_ref[...], (G, TAXO))
    level_row = lax.broadcasted_iota(jnp.int32, (G, TAXO), 0)
    for bit in range(5):
        size = 1 << bit
        moved = jnp.where(level_row >= size, pltpu.roll(table, size, 0), 0.0)
        table = jnp.where((offset & size) != 0, moved, table)
    measure = jnp.broadcast_to(measure_ref[...], (G, TAXO))
    both = jnp.concatenate(
        [jnp.where(measure == 0, table, 0.0), jnp.where(measure == 1, table, 0.0)], axis=0
    )
    curve_s[...] = both.T
    curve_ref[...] = curve_s[pl.ds(pl.multiple_of(first, ROWS), t_dev), :].astype(BF16)


def swap_groups(block, groups, width):
    total = block.shape[0]
    high = total // groups
    row_group = lax.broadcasted_iota(jnp.int32, block.shape, 0) // high
    lane_group = lax.broadcasted_iota(jnp.int32, block.shape, 1) // width
    result = block
    for d in range(1, groups):
        moved = pltpu.roll(pltpu.roll(block, total - high * d, 0), width * d, 1)
        gap = lane_group - row_group
        result = jnp.where((gap == d) | (gap == d - groups), moved, result)
    return result


def loss_kernel(n_ev, n_site, n_rup, got_ref, coords_ref, exp_ref, curve_ref, out_ref, geo_s, ratio_s, loss_s):
    n_dev = n_ev * n_site
    t_dev = curve_ref.shape[0]
    n_col = exp_ref.shape[1]
    events = n_dev
    ev_dev = events // n_ev
    me = lax.axis_index("site")
    start = pl.multiple_of(me * SITE_DEV, LANES)
    x = coords_ref[0:1, pl.ds(start, SITE_DEV)]
    y = coords_ref[1:2, pl.ds(start, SITE_DEV)]

    every = got_ref[:, :, SITE_DEV:].astype(F32)[:, 0, :]
    geo_s[...] = every
    table = jnp.concatenate(
        [
            every if u == 0 and p == 0 else pltpu.roll(every, LANES - 6 * u - PART * p, 1)
            for p in range(3)
            for u in range(n_rup)
        ],
        axis=0,
    ).astype(BF16)
    level = lax.broadcasted_iota(jnp.int32, (G, SITE_DEV), 0).astype(F32).astype(BF16)
    level_less = (lax.broadcasted_iota(jnp.int32, (G, SITE_DEV), 0) - 1).astype(F32).astype(BF16)
    zero = jnp.zeros((G, SITE_DEV), BF16)
    curve = curve_ref[...]
    exposure = exp_ref[...]
    diagonal = lax.broadcasted_iota(jnp.int32, (t_dev, n_col), 0) == (
        lax.broadcasted_iota(jnp.int32, (t_dev, n_col), 1) % t_dev
    )

    def joined(array):
        return (array + pltpu.roll(array, LANES - PART, 1)) + pltpu.roll(array, LANES - 2 * PART, 1)

    def block(b, carry):
        first = pl.multiple_of(b * EVENT_BLOCK, EVENT_BLOCK)
        here = joined(geo_s[pl.ds(first, EVENT_BLOCK), :])
        rupture = here[:, 6 * n_rup : 6 * n_rup + 1].astype(jnp.int32)
        place = lax.broadcasted_iota(jnp.int32, (EVENT_BLOCK, n_dev), 1) * n_rup
        hot = jnp.concatenate([(place + u == rupture).astype(BF16) for u in range(n_rup)] * 3, axis=1)
        own = jnp.dot(hot, table, preferred_element_type=F32)
        start_x = own[:, 0:1]
        start_y = own[:, 1:2]
        along_x = own[:, 2:3] - start_x
        along_y = own[:, 3:4] - start_y
        depth = own[:, 4:5]
        size = own[:, 5:6]
        length_sq = along_x * along_x + along_y * along_y
        rel_x = x - start_x
        rel_y = y - start_y
        portion = jnp.clip((rel_x * along_x + rel_y * along_y) / length_sq, 0.0, 1.0)
        off_x = rel_x - portion * along_x
        off_y = rel_y - portion * along_y
        distance = jnp.sqrt(off_x * off_x + off_y * off_y + depth * depth)
        got = got_ref[pl.ds(b * EVENT_BLOCK, EVENT_BLOCK), :, :SITE_DEV].astype(F32)
        below, weight_0, weight_1 = [], [], []
        for k in range(2):
            c = COEFFS[k]
            eps = got[:, k, :]
            field = (
                c[0] + c[1] * (size - 6.0)
                - c[2] * 0.5 * jnp.log(distance * distance + c[3] * c[3])
                - c[4] * distance
                + c[5] * eps
            )
            position = jnp.clip((field - LOW_LEVEL) / LEVEL_STEP, 0.0, G - 1.0)
            floor = jnp.floor(position)
            below.append(floor.astype(BF16))
            weight_0.append((1.0 - (position - floor)).astype(BF16))
            weight_1.append(jnp.maximum(0.0, 1.0 - ((floor + 1.0) - position)).astype(BF16))

        def wide(array, e):
            return jnp.broadcast_to(array[e : e + 1], (G, SITE_DEV))

        ratios = []
        for e in range(EVENT_BLOCK):
            tents = []
            for k in range(2):
                at = wide(below[k], e)
                tents.append(
                    jnp.where(
                        level == at,
                        wide(weight_0[k], e),
                        jnp.where(level_less == at, wide(weight_1[k], e), zero),
                    )
                )
            ratio = jnp.dot(curve, jnp.concatenate(tents, axis=0), preferred_element_type=F32)
            ratios.append(ratio.astype(BF16))
            if len(ratios) * t_dev == 32:
                ratio_s[(e + 1) * t_dev - 32 : (e + 1) * t_dev, :] = jnp.concatenate(ratios, axis=0)
                ratios = []
        terms = jnp.dot(ratio_s[...], exposure, preferred_element_type=F32)
        rows = [
            jnp.sum(jnp.where(diagonal, terms[e * t_dev : (e + 1) * t_dev], 0.0), axis=0, keepdims=True)
            for e in range(EVENT_BLOCK)
        ]
        loss_s[pl.ds(first, EVENT_BLOCK), :] = jnp.concatenate(rows, axis=0)
        return carry

    lax.fori_loop(0, events // EVENT_BLOCK, block, 0)

    halves = n_col // LANES

    def arrange(i, carry):
        first = pl.multiple_of(i * ev_dev, ROWS)
        for u in range(halves):
            part = loss_s[pl.ds(first, ev_dev), u * LANES : (u + 1) * LANES]
            out_ref[pl.ds(pl.multiple_of((i * halves + u) * ev_dev, ROWS), ev_dev), :] = swap_groups(
                part, n_ev, t_dev
            )
        return carry

    lax.fori_loop(0, n_ev, arrange, 0, unroll=n_ev <= 4)


def total_kernel(n_ev, n_site, got_ref, out_ref):
    each = got_ref.shape[0] // n_ev
    high = each // n_site
    row_group = lax.broadcasted_iota(jnp.int32, (ROWS, LANES), 0) // high
    blocks = []
    for i in range(n_ev):
        part = got_ref[i * each : i * each + ROWS, :]
        for q in range(ROWS, each, ROWS):
            part = part + got_ref[i * each + q : i * each + q + ROWS, :]
        move = ROWS // 2
        while move >= high:
            part = part + pltpu.roll(part, move, 0)
            move //= 2
        if i % (ROWS // high) == 0:
            blocks.append(part)
        else:
            blocks[-1] = jnp.where(row_group == i % (ROWS // high), part, blocks[-1])
    out_ref[...] = swap_groups(jnp.concatenate(blocks, axis=0), n_ev, LANES // n_ev)


def shards(
    ruptures,
    event_rupture,
    epsilon,
    site_coords,
    vulnerability,
    taxo_measure,
    taxo_offset,
    asset_site,
    asset_taxo,
    asset_tract,
    asset_value,
):
    n_ev = lax.axis_size("ev")
    n_site = lax.axis_size("site")
    n_dev = n_ev * n_site
    n_rup = ruptures.shape[1]
    sites = epsilon.shape[2]
    t_dev = TAXO // n_ev
    n_col = n_site * t_dev
    asset_rows = asset_site.shape[0] // LANES

    def stays(array):
        return pltpu.with_memory_space_constraint(array, pltpu.HBM)

    def exchange(array):
        return lax.all_to_all(array, AXES, split_axis=0, concat_axis=0, tiled=True)

    place = pl.pallas_call(
        place_kernel,
        out_shape=jax.ShapeDtypeStruct((ROWS, LANES), jnp.int32),
        out_specs=VMEM,
        compiler_params=params(4),
        cost_estimate=pl.CostEstimate(flops=4_000_000_000, bytes_accessed=12_000_000, transcendentals=0),
    )()
    packed = pl.pallas_call(
        lambda *refs: pack_kernel(n_ev, n_site, *refs),
        out_shape=jax.ShapeDtypeStruct((n_dev, 2, SITE_DEV + LANES), BF16),
        in_specs=[VMEM, VMEM, SMEM, VMEM],
        out_specs=VMEM,
        compiler_params=params(4),
    )(place, ruptures, event_rupture, epsilon.reshape(2, sites))
    got = exchange(packed)

    def as_rows(array):
        return array.reshape(asset_rows, LANES)

    exposure, curve = pl.pallas_call(
        lambda *refs: exposure_kernel(t_dev, COMPACT_ROWS, *refs),
        out_shape=(
            jax.ShapeDtypeStruct((SITE_DEV, n_col), BF16),
            jax.ShapeDtypeStruct((t_dev, 2 * G), BF16),
        ),
        in_specs=[VMEM] * 4 + [HBM] * 3,
        out_specs=(VMEM, VMEM),
        scratch_shapes=[pltpu.VMEM((asset_rows, LANES), F32)] * 4
        + [pltpu.VMEM((SITE_DEV, n_col), F32), pltpu.VMEM((TAXO, 2 * G), F32)]
        + [pltpu.VMEM((NB, TAXO), BF16), pltpu.VMEM((1, TAXO), jnp.int32), pltpu.VMEM((1, TAXO), jnp.int32)]
        + [pltpu.SemaphoreType.DMA((3,))],
        compiler_params=params(24),
        cost_estimate=pl.CostEstimate(
            flops=2 * asset_rows * LANES * SITE_DEV * n_col, bytes_accessed=1 << 20, transcendentals=0
        ),
    )(
        as_rows(asset_site),
        as_rows(asset_taxo),
        as_rows(asset_tract),
        as_rows(asset_value),
        stays(vulnerability.T),
        stays(taxo_measure.reshape(1, TAXO)),
        stays(taxo_offset.reshape(1, TAXO)),
    )

    parts = pl.pallas_call(
        lambda *refs: loss_kernel(n_ev, n_site, n_rup, *refs),
        out_shape=jax.ShapeDtypeStruct((n_dev * n_col // LANES, LANES), F32),
        in_specs=[VMEM] * 4,
        out_specs=VMEM,
        scratch_shapes=[
            pltpu.VMEM((n_dev, LANES), F32),
            pltpu.VMEM((EVENT_BLOCK * t_dev, SITE_DEV), BF16),
            pltpu.VMEM((n_dev, n_col), F32),
        ],
        compiler_params=params(20),
    )(got, site_coords, exposure, curve)

    losses = pl.pallas_call(
        lambda *refs: total_kernel(n_ev, n_site, *refs),
        out_shape=jax.ShapeDtypeStruct((n_dev // n_ev, LANES), F32),
        in_specs=[VMEM],
        out_specs=VMEM,
        compiler_params=params(4),
    )(exchange(parts))
    return losses[None]


def solution(mesh):
    in_specs = (
        P(None, ("ev", "site")),
        P(("ev", "site")),
        P(None, ("ev", "site"), None),
        P(),
        P(),
        P(),
        P(),
        P("site"),
        P("site"),
        P("site"),
        P("site"),
    )
    out_specs = P("site", "ev", None)
    return jax.shard_map(shards, mesh=mesh, in_specs=in_specs, out_specs=out_specs, check_vma=False)
```

```python
import jax
import jax.numpy as jnp
from jax import lax
from jax.experimental import pallas as pl
from jax.experimental.pallas import tpu as pltpu
from jax.sharding import PartitionSpec as P

SITE_DEV = 512
TAXO = 128
G = 64
NB = 40
LANES = 128
ROWS = 8
PART = 16
EVENT_BLOCK = 32
CODES = 1 << 17
SLANT = 13
HOLE = 1 << 24
COMPACT_ROWS = 10

COEFFS = ((1.0, 1.1, 1.0, 6.0, 0.004, 0.6), (0.3, 1.4, 0.9, 8.0, 0.002, 0.7))
LOW_LEVEL = -6.0
LEVEL_STEP = 0.1

AXES = ("ev", "site")
F32 = jnp.float32
BF16 = jnp.bfloat16
NT = (((1,), (1,)), ((), ()))

VMEM = pl.BlockSpec(memory_space=pltpu.VMEM)
SMEM = pl.BlockSpec(memory_space=pltpu.SMEM)
HBM = pl.BlockSpec(memory_space=pltpu.HBM)


def params(mebibytes):
    return pltpu.CompilerParams(vmem_limit_bytes=mebibytes << 20)


def parts_of(value):
    high = value.astype(BF16).astype(F32)
    rest = value - high
    middle = rest.astype(BF16).astype(F32)
    return high, middle, (rest - middle).astype(BF16).astype(F32)


def place_kernel(out_ref):
    out_ref[...] = lax.broadcasted_iota(jnp.int32, out_ref.shape, 1) - lax.broadcasted_iota(
        jnp.int32, out_ref.shape, 0
    )


def pack_kernel(n_ev, n_site, place_ref, rup_ref, idx_ref, eps_ref, out_ref):
    n_rup = rup_ref.shape[1]
    place = place_ref[0:6, :]
    spots = jnp.zeros((6, LANES), F32)
    for k in range(n_rup):
        spots = jnp.where(place == 6 * k, jnp.broadcast_to(rup_ref[:, k : k + 1], (6, LANES)), spots)
    row = jnp.broadcast_to(jnp.sum(spots, axis=0, keepdims=True), (2, LANES))
    lane = jnp.broadcast_to(place_ref[0:1, :], (2, LANES))
    row = jnp.where(lane == 6 * n_rup, idx_ref[0].astype(F32), row)
    high, middle, low = parts_of(row)
    row = (high + pltpu.roll(middle, PART, 1) + pltpu.roll(low, 2 * PART, 1)).astype(BF16)
    eps = eps_ref[...]

    def fill(i, carry):
        for j in range(n_site):
            own = eps[:, j * SITE_DEV : (j + 1) * SITE_DEV]
            out_ref[i * n_site + j] = jnp.concatenate([own, row], axis=1)
        return carry

    lax.fori_loop(0, n_ev, fill, 0, unroll=n_ev <= 4)


def compact(own, code, value):
    rows = own.shape[0]
    above = lax.broadcasted_iota(jnp.int32, (rows, rows), 1) < lax.broadcasted_iota(jnp.int32, (rows, rows), 0)
    gaps = jnp.dot(above.astype(BF16), 1.0 - own.astype(BF16), preferred_element_type=F32).astype(jnp.int32)
    word = jnp.where(own, gaps * CODES + code, HOLE)
    size = 1
    while size < rows:
        bit = size * CODES
        from_word = jnp.concatenate([word[size:], jnp.full((size, LANES), HOLE, jnp.int32)], axis=0)
        from_value = jnp.concatenate([value[size:], jnp.zeros((size, LANES), F32)], axis=0)
        comes = (from_word & bit) != 0
        value = jnp.where(comes, from_value, value)
        word = jnp.where(comes, from_word, jnp.where((word & bit) != 0, HOLE, word))
        size *= 2
    return word, value


def slanted(array):
    return jnp.concatenate(
        [
            pltpu.roll(array[q : q + ROWS], (11 * q // ROWS) % 36, 1, stride=SLANT, stride_axis=0)
            for q in range(0, array.shape[0], ROWS)
        ],
        axis=0,
    )


def exposure_kernel(
    t_dev, rows, site_ref, taxo_ref, tract_ref, value_ref, vul_hbm, measure_hbm, offset_hbm,
    exp_ref, curve_ref, site_s, col_s, high_s, low_s, sum_s, curve_s, vul_ref, measure_ref, offset_ref, sems,
):
    copies = [
        pltpu.make_async_copy(source, target, sems.at[k])
        for k, (source, target) in enumerate(
            ((vul_hbm, vul_ref), (measure_hbm, measure_ref), (offset_hbm, offset_ref))
        )
    ]
    for copy in copies:
        copy.start()
    me = lax.axis_index("ev")
    first = me * t_dev
    n_col = exp_ref.shape[1]
    taxo = taxo_ref[...] - first
    own = (taxo >= 0) & (taxo < t_dev)
    code = site_ref[...] * n_col + tract_ref[...] * t_dev + taxo
    word, value = compact(own, code, value_ref[...])
    word, value = slanted(word), slanted(value)
    own = word != HOLE
    most = jnp.max(jnp.sum(own.astype(F32), axis=0, keepdims=True)).astype(jnp.int32)
    word, value = compact(own, word & (CODES - 1), value)
    high = value.astype(BF16).astype(F32)
    site_s[...] = ((word & (CODES - 1)) // n_col).astype(F32)
    col_s[...] = jnp.where((word & HOLE) != 0, -1, word & (n_col - 1)).astype(F32)
    high_s[...] = high
    low_s[...] = value - high

    level = lax.broadcasted_iota(jnp.int32, (256, LANES), 0).astype(F32).astype(BF16)
    zero = jnp.zeros((256, LANES), BF16)
    one = jnp.ones((256, LANES), BF16)

    def spread(ref, q, less=0.0):
        return jnp.broadcast_to((ref[pl.ds(q, 1), :] - less).astype(BF16), (256, LANES))

    def beside(parts):
        return jnp.concatenate(parts, axis=1)

    sum_s[...] = jnp.zeros_like(sum_s)

    def step(c, carry):
        site_rows = [[] for _ in range(SITE_DEV // 256)]
        high_rows, low_rows = [], []
        for u in range(rows):
            q = c * rows + u
            for part, found in enumerate(site_rows):
                found.append(jnp.where(level == spread(site_s, q, 256.0 * part), one, zero))
            here = level == spread(col_s, q)
            high_rows.append(jnp.where(here, spread(high_s, q), zero))
            low_rows.append(jnp.where(here, spread(low_s, q), zero))
        at_site = jnp.concatenate([beside(found) for found in site_rows], axis=0)
        sum_s[...] += lax.dot_general(
            beside([at_site, at_site]), beside(high_rows + low_rows), NT, preferred_element_type=F32
        )
        return carry

    lax.fori_loop(0, (most + rows - 1) // rows, step, 0)
    exp_ref[...] = sum_s[...].astype(BF16)

    for copy in copies:
        copy.wait()
    vul = vul_ref[...].astype(F32)
    table = jnp.concatenate([vul, jnp.broadcast_to(vul[NB - 1 : NB], (G - NB, TAXO))], axis=0)
    offset = jnp.broadcast_to(offset_ref[...], (G, TAXO))
    level_row = lax.broadcasted_iota(jnp.int32, (G, TAXO), 0)
    for bit in range(5):
        size = 1 << bit
        moved = jnp.where(level_row >= size, pltpu.roll(table, size, 0), 0.0)
        table = jnp.where((offset & size) != 0, moved, table)
    measure = jnp.broadcast_to(measure_ref[...], (G, TAXO))
    both = jnp.concatenate(
        [jnp.where(measure == 0, table, 0.0), jnp.where(measure == 1, table, 0.0)], axis=0
    )
    curve_s[...] = both.T
    curve_ref[...] = curve_s[pl.ds(pl.multiple_of(first, ROWS), t_dev), :].astype(BF16)


def swap_groups(block, groups, width):
    total = block.shape[0]
    high = total // groups
    row_group = lax.broadcasted_iota(jnp.int32, block.shape, 0) // high
    lane_group = lax.broadcasted_iota(jnp.int32, block.shape, 1) // width
    result = block
    for d in range(1, groups):
        moved = pltpu.roll(pltpu.roll(block, total - high * d, 0), width * d, 1)
        gap = lane_group - row_group
        result = jnp.where((gap == d) | (gap == d - groups), moved, result)
    return result


def loss_kernel(n_ev, n_site, n_rup, got_ref, coords_ref, exp_ref, curve_ref, out_ref, geo_s, ratio_s, loss_s):
    n_dev = n_ev * n_site
    t_dev = curve_ref.shape[0]
    n_col = exp_ref.shape[1]
    events = n_dev
    ev_dev = events // n_ev
    me = lax.axis_index("site")
    start = pl.multiple_of(me * SITE_DEV, LANES)
    x = coords_ref[0:1, pl.ds(start, SITE_DEV)]
    y = coords_ref[1:2, pl.ds(start, SITE_DEV)]

    every = got_ref[:, :, SITE_DEV:].astype(F32)[:, 0, :]
    geo_s[...] = every
    table = jnp.concatenate(
        [
            every if u == 0 and p == 0 else pltpu.roll(every, LANES - 6 * u - PART * p, 1)
            for p in range(3)
            for u in range(n_rup)
        ],
        axis=0,
    ).astype(BF16)
    level = lax.broadcasted_iota(jnp.int32, (G, SITE_DEV), 0).astype(F32).astype(BF16)
    level_less = (lax.broadcasted_iota(jnp.int32, (G, SITE_DEV), 0) - 1).astype(F32).astype(BF16)
    zero = jnp.zeros((G, SITE_DEV), BF16)
    curve = curve_ref[...]
    exposure = exp_ref[...]
    own_taxo = lax.broadcasted_iota(jnp.int32, (ROWS, n_col), 1) % t_dev
    diagonal = lax.broadcasted_iota(jnp.int32, (ROWS, n_col), 0) == own_taxo % ROWS
    taxo_rows = own_taxo // ROWS

    def joined(array):
        return (array + pltpu.roll(array, LANES - PART, 1)) + pltpu.roll(array, LANES - 2 * PART, 1)

    def block(b, carry):
        first = pl.multiple_of(b * EVENT_BLOCK, EVENT_BLOCK)
        here = joined(geo_s[pl.ds(first, EVENT_BLOCK), :])
        rupture = here[:, 6 * n_rup : 6 * n_rup + 1].astype(jnp.int32)
        place = lax.broadcasted_iota(jnp.int32, (EVENT_BLOCK, n_dev), 1) * n_rup
        hot = jnp.concatenate([(place + u == rupture).astype(BF16) for u in range(n_rup)] * 3, axis=1)
        own = jnp.dot(hot, table, preferred_element_type=F32)
        start_x = own[:, 0:1]
        start_y = own[:, 1:2]
        along_x = own[:, 2:3] - start_x
        along_y = own[:, 3:4] - start_y
        depth = own[:, 4:5]
        size = own[:, 5:6]
        length_sq = along_x * along_x + along_y * along_y
        rel_x = x - start_x
        rel_y = y - start_y
        portion = jnp.clip((rel_x * along_x + rel_y * along_y) / length_sq, 0.0, 1.0)
        off_x = rel_x - portion * along_x
        off_y = rel_y - portion * along_y
        distance = jnp.sqrt(off_x * off_x + off_y * off_y + depth * depth)
        got = got_ref[pl.ds(b * EVENT_BLOCK, EVENT_BLOCK), :, :SITE_DEV].astype(F32)
        below, weight_0, weight_1 = [], [], []
        for k in range(2):
            c = COEFFS[k]
            eps = got[:, k, :]
            field = (
                c[0] + c[1] * (size - 6.0)
                - c[2] * 0.5 * jnp.log(distance * distance + c[3] * c[3])
                - c[4] * distance
                + c[5] * eps
            )
            position = jnp.clip((field - LOW_LEVEL) / LEVEL_STEP, 0.0, G - 1.0)
            floor = jnp.floor(position)
            below.append(floor.astype(BF16))
            weight_0.append((1.0 - (position - floor)).astype(BF16))
            weight_1.append(jnp.maximum(0.0, 1.0 - ((floor + 1.0) - position)).astype(BF16))

        def wide(array, e):
            return jnp.broadcast_to(array[e : e + 1], (G, SITE_DEV))

        ratios = []
        for e in range(EVENT_BLOCK):
            tents = []
            for k in range(2):
                at = wide(below[k], e)
                tents.append(
                    jnp.where(
                        level == at,
                        wide(weight_0[k], e),
                        jnp.where(level_less == at, wide(weight_1[k], e), zero),
                    )
                )
            ratio = jnp.dot(curve, jnp.concatenate(tents, axis=0), preferred_element_type=F32)
            ratios.append(ratio.astype(BF16))
            if len(ratios) * t_dev == 32:
                ratio_s[(e + 1) * t_dev - 32 : (e + 1) * t_dev, :] = jnp.concatenate(ratios, axis=0)
                ratios = []
        terms = jnp.dot(ratio_s[...], exposure, preferred_element_type=F32)
        rows = []
        for e in range(EVENT_BLOCK):
            part = terms[e * t_dev : e * t_dev + ROWS]
            for q in range(1, t_dev // ROWS):
                part = jnp.where(taxo_rows == q, terms[e * t_dev + q * ROWS : e * t_dev + (q + 1) * ROWS], part)
            rows.append(jnp.sum(jnp.where(diagonal, part, 0.0), axis=0, keepdims=True))
        loss_s[pl.ds(first, EVENT_BLOCK), :] = jnp.concatenate(rows, axis=0)
        return carry

    lax.fori_loop(0, events // EVENT_BLOCK, block, 0)

    halves = n_col // LANES

    def arrange(i, carry):
        first = pl.multiple_of(i * ev_dev, ROWS)
        for u in range(halves):
            part = loss_s[pl.ds(first, ev_dev), u * LANES : (u + 1) * LANES]
            out_ref[pl.ds(pl.multiple_of((i * halves + u) * ev_dev, ROWS), ev_dev), :] = swap_groups(
                part, n_ev, t_dev
            )
        return carry

    lax.fori_loop(0, n_ev, arrange, 0, unroll=n_ev <= 4)


def total_kernel(n_ev, n_site, got_ref, out_ref):
    each = got_ref.shape[0] // n_ev
    high = each // n_site
    row_group = lax.broadcasted_iota(jnp.int32, (ROWS, LANES), 0) // high
    blocks = []
    for i in range(n_ev):
        part = got_ref[i * each : i * each + ROWS, :]
        for q in range(ROWS, each, ROWS):
            part = part + got_ref[i * each + q : i * each + q + ROWS, :]
        move = ROWS // 2
        while move >= high:
            part = part + pltpu.roll(part, move, 0)
            move //= 2
        if i % (ROWS // high) == 0:
            blocks.append(part)
        else:
            blocks[-1] = jnp.where(row_group == i % (ROWS // high), part, blocks[-1])
    out_ref[...] = swap_groups(jnp.concatenate(blocks, axis=0), n_ev, LANES // n_ev)


def shards(
    ruptures,
    event_rupture,
    epsilon,
    site_coords,
    vulnerability,
    taxo_measure,
    taxo_offset,
    asset_site,
    asset_taxo,
    asset_tract,
    asset_value,
):
    n_ev = lax.axis_size("ev")
    n_site = lax.axis_size("site")
    n_dev = n_ev * n_site
    n_rup = ruptures.shape[1]
    sites = epsilon.shape[2]
    t_dev = TAXO // n_ev
    n_col = n_site * t_dev
    asset_rows = asset_site.shape[0] // LANES

    def stays(array):
        return pltpu.with_memory_space_constraint(array, pltpu.HBM)

    def exchange(array):
        return lax.all_to_all(array, AXES, split_axis=0, concat_axis=0, tiled=True)

    place = pl.pallas_call(
        place_kernel,
        out_shape=jax.ShapeDtypeStruct((ROWS, LANES), jnp.int32),
        out_specs=VMEM,
        compiler_params=params(4),
        cost_estimate=pl.CostEstimate(flops=4_000_000_000, bytes_accessed=12_000_000, transcendentals=0),
    )()
    packed = pl.pallas_call(
        lambda *refs: pack_kernel(n_ev, n_site, *refs),
        out_shape=jax.ShapeDtypeStruct((n_dev, 2, SITE_DEV + LANES), BF16),
        in_specs=[VMEM, VMEM, SMEM, VMEM],
        out_specs=VMEM,
        compiler_params=params(4),
    )(place, ruptures, event_rupture, epsilon.reshape(2, sites))
    got = exchange(packed)

    def as_rows(array):
        return array.reshape(asset_rows, LANES)

    exposure, curve = pl.pallas_call(
        lambda *refs: exposure_kernel(t_dev, COMPACT_ROWS, *refs),
        out_shape=(
            jax.ShapeDtypeStruct((SITE_DEV, n_col), BF16),
            jax.ShapeDtypeStruct((t_dev, 2 * G), BF16),
        ),
        in_specs=[VMEM] * 4 + [HBM] * 3,
        out_specs=(VMEM, VMEM),
        scratch_shapes=[pltpu.VMEM((asset_rows, LANES), F32)] * 4
        + [pltpu.VMEM((SITE_DEV, n_col), F32), pltpu.VMEM((TAXO, 2 * G), F32)]
        + [pltpu.VMEM((NB, TAXO), BF16), pltpu.VMEM((1, TAXO), jnp.int32), pltpu.VMEM((1, TAXO), jnp.int32)]
        + [pltpu.SemaphoreType.DMA((3,))],
        compiler_params=params(24),
        cost_estimate=pl.CostEstimate(
            flops=2 * asset_rows * LANES * SITE_DEV * n_col, bytes_accessed=1 << 20, transcendentals=0
        ),
    )(
        as_rows(asset_site),
        as_rows(asset_taxo),
        as_rows(asset_tract),
        as_rows(asset_value),
        stays(vulnerability.T),
        stays(taxo_measure.reshape(1, TAXO)),
        stays(taxo_offset.reshape(1, TAXO)),
    )

    parts = pl.pallas_call(
        lambda *refs: loss_kernel(n_ev, n_site, n_rup, *refs),
        out_shape=jax.ShapeDtypeStruct((n_dev * n_col // LANES, LANES), F32),
        in_specs=[VMEM] * 4,
        out_specs=VMEM,
        scratch_shapes=[
            pltpu.VMEM((n_dev, LANES), F32),
            pltpu.VMEM((EVENT_BLOCK * t_dev, SITE_DEV), BF16),
            pltpu.VMEM((n_dev, n_col), F32),
        ],
        compiler_params=params(20),
    )(got, site_coords, exposure, curve)

    losses = pl.pallas_call(
        lambda *refs: total_kernel(n_ev, n_site, *refs),
        out_shape=jax.ShapeDtypeStruct((n_dev // n_ev, LANES), F32),
        in_specs=[VMEM],
        out_specs=VMEM,
        compiler_params=params(4),
    )(exchange(parts))
    return losses[None]


def solution(mesh):
    in_specs = (
        P(None, ("ev", "site")),
        P(("ev", "site")),
        P(None, ("ev", "site"), None),
        P(),
        P(),
        P(),
        P(),
        P("site"),
        P("site"),
        P("site"),
        P("site"),
    )
    out_specs = P("site", "ev", None)
    return jax.shard_map(shards, mesh=mesh, in_specs=in_specs, out_specs=out_specs, check_vma=False)
```
